512 devices in a mesh: section: 64 (over y, z_hi, x), dp: 8 (over z_lo, core).
Axes of the slice: x: 4, y: 4, z: 16 (z_hi: 4, z_lo: 4; z = z_hi * 4 + z_lo), core: 2. Of those that a mesh axis runs over, the one named last changes fastest.
Arguments:
- x_saved: bfloat16 [4, 256, 16384], P(None, 'dp', 'section'), may hold values from -6 to 6
- side_grad: bfloat16 [4, 256, 16384], P(None, 'dp', 'section'), may hold values from -4 to 4
- plan: int32 [4], replicated, may hold values from 0 to 3, each once
- w_low: bfloat16 [16384, 512], P('section'), may hold values from -0.0625 to 0.0625
- w_delta: bfloat16 [512, 16384], P(None, 'section'), may hold values from -0.25 to 0.25
- w_select: bfloat16 [32, 16384], P(None, 'section'), may hold values from -0.015625 to 0.015625
- decay_rate: float32 [16, 16384], P(None, 'section'), may hold values from 0.1 to 16
- delta_bias: float32 [16384], P('section'), may hold values from -4 to -1
- skip_gain: float32 [16384], P('section'), may hold values from -0.25 to 0.25
Outputs:
- grad_inputs: bfloat16 [4, 256, 16384], P(None, 'dp', 'section')
- grad_low: float32 [16384, 512], P(('section', 'dp'))
- grad_delta: float32 [512, 16384], P('dp', 'section')
- grad_select: float32 [32, 16384], P('dp', 'section')
- grad_rate: float32 [16, 16384], P('dp', 'section')
- grad_bias: float32 [16384], P(('section', 'dp'))
- grad_skip: float32 [16384], P(('section', 'dp'))
The draws below stay inside these ranges and needn't reach their ends.
Inputs may be any that keep to these rules, and one draw needn't show every extreme that they name: `plan`: each micro-batch appears exactly once.
All inputs are finite; a program needn't handle non-finite values.
Results may differ from the reference program's by a relative error of at most 0.03.
Values may be sent and summed in bfloat16 or wider, within the bound.
No kernel may reach another device: no remote copies, remote signals or barrier semaphores. Data moves between devices by JAX's collectives and lax.ppermute only.
A program may use at most 64 MiB of HBM per device.

```python
import math
import jax
import jax.numpy as jnp
from jax import lax

CH = 8192
RANK = 512
NST = 16
LAYERS = 2
LEN = 32
MB = 4
TOKENS = 256
N_DP = 8


def levels(rng, extent, pieces, smallest, largest):
    factor_of, own = 1.0, jax.random.fold_in(rng, 6)
    for axis_at, shards_of in pieces:
        heights = jnp.exp(jax.random.uniform(jax.random.fold_in(own, axis_at), (shards_of,), jnp.float32, smallest / len(pieces), largest / len(pieces)))
        factor_of = factor_of * jnp.repeat(heights, extent[axis_at] // shards_of).reshape([-1 if axis == axis_at else 1 for axis in range(len(extent))])
    return factor_of


def scatter_about(own_key, dims, width, reach, split=(), held_as=jnp.bfloat16):
    values = width * jax.random.normal(own_key, dims, jnp.float32)
    if split:
        values = values * levels(own_key, dims, split, -0.22, 0.18)
    return jnp.clip(values, -reach, reach).astype(held_as)


def setup_inputs(seed: int = 0) -> dict:
    key_list = jax.random.split(jax.random.key(seed), 10)
    return {
        "x_saved": scatter_about(key_list[0], (MB, TOKENS, LAYERS * CH), 1.0, 6.0, ((1, 8), (2, 64))),
        "side_grad": scatter_about(key_list[1], (MB, TOKENS, LAYERS * CH), 0.5, 4.0, ((1, 8), (2, 64))),
        "plan": jax.random.permutation(key_list[2], MB).astype(jnp.int32),
        "w_low": scatter_about(key_list[3], (LAYERS * CH, RANK), CH ** -0.5, 0.0625, ((0, 64),)),
        "w_delta": scatter_about(key_list[4], (RANK, LAYERS * CH), RANK ** -0.5, 0.25, ((1, 64),)),
        "w_select": scatter_about(key_list[5], (2 * NST, LAYERS * CH), (16 * CH) ** -0.5, 0.015625, ((1, 64),)),
        "decay_rate": jnp.clip(jnp.exp(math.log(16.0) - 5.075174 * jax.random.uniform(key_list[6], (NST, LAYERS * CH), jnp.float32) ** levels(key_list[6], (NST, LAYERS * CH), ((1, 64),), -0.2, 0.2)), 0.1, 16.0),
        "delta_bias": jnp.clip(-4.0 + 3.0 * jax.random.uniform(key_list[7], (LAYERS * CH,), jnp.float32) ** levels(key_list[7], (LAYERS * CH,), ((0, 64),), -0.2, 0.2), -4.0, -1.0),
        "skip_gain": jnp.clip(jax.random.uniform(key_list[8], (LAYERS * CH,), jnp.float32, -0.25, 0.25) * levels(key_list[8], (LAYERS * CH,), ((0, 64),), -0.4, 0.0), -0.25, 0.25),
    }


def combine(earlier, later_pair):
    return (earlier[0] * later_pair[0], later_pair[0] * earlier[1] + later_pair[1])

def scan_core(x_float, step_size, b_proj, c_proj, rate_table, gain_vector):
    decays = jnp.exp(-step_size[:, None, :] * rate_table[None, :, :])
    driven = b_proj[:, :, None] * (step_size * x_float)[:, None, :]
    _, states = lax.associative_scan(combine, (decays, driven), axis=0)
    return jnp.einsum('lnc,ln->lc', states, c_proj) + gain_vector * x_float

def section_backward(x_rows, grad_out, w_lowrank, w_step, w_proj, rate_table, biases, gain_vector):
    state_count = w_proj.shape[0] // 2
    lowrank = jnp.dot(x_rows, w_lowrank, preferred_element_type=jnp.float32).astype(jnp.bfloat16)
    selected = lax.dot_general(x_rows, w_proj, (((1,), (1,)), ((), ())), preferred_element_type=jnp.float32)
    pre_act = jnp.dot(lowrank, w_step, preferred_element_type=jnp.float32) + biases
    step_size = jax.nn.softplus(pre_act)
    x_float = x_rows.astype(jnp.float32)
    _, pullback = jax.vjp(scan_core, x_float, step_size, selected[:, :state_count], selected[:, state_count:], rate_table, gain_vector)
    grad_core, grad_step, grad_bsel, grad_csel, rate_part, skip_part = pullback(grad_out)
    dpre = grad_step * jax.nn.sigmoid(pre_act)
    dpre_half = dpre.astype(jnp.bfloat16)
    dsel_half = jnp.concatenate([grad_bsel, grad_csel], axis=1).astype(jnp.bfloat16)
    dlow_half = lax.dot_general(dpre_half, w_step, (((1,), (1,)), ((), ())), preferred_element_type=jnp.float32).astype(jnp.bfloat16)
    summed_grad = grad_out + grad_core
    summed_grad = summed_grad + lax.dot_general(dlow_half, w_lowrank, (((1,), (1,)), ((), ())), preferred_element_type=jnp.float32)
    summed_grad = summed_grad + jnp.dot(dsel_half, w_proj, preferred_element_type=jnp.float32)
    return (summed_grad.astype(jnp.bfloat16), lowrank, dpre_half, dlow_half, dsel_half, rate_part, lax.optimization_barrier(jnp.sum(dpre, axis=0)), skip_part)

def reference(x_saved, side_grad, plan, w_low, w_delta, w_select, decay_rate, delta_bias, skip_gain):

    def by_layer(array):
        return array.reshape(MB, N_DP, LEN, LAYERS, CH).transpose(3, 0, 1, 2, 4).reshape(LAYERS, MB * N_DP, LEN, CH)

    def lead(array, rows):
        return array.reshape(rows, LAYERS, CH).transpose(1, 0, 2)

    def unlead(array):
        return array.transpose(1, 0, 2).reshape(array.shape[1], LAYERS * CH)

    def per_replica(array):
        return array.reshape((MB, N_DP) + array.shape[1:]).astype(jnp.float32)

    def combine_replicas(partial_sum):
        rounded = lax.optimization_barrier(partial_sum.astype(jnp.bfloat16))
        return lax.optimization_barrier(jnp.sum(rounded.astype(jnp.float32), axis=0))

    def one_section(grad_above, packed):
        x_layer, side_layer, w_lowrank, w_step, w_proj, rate_table, biases, gain_vector = packed
        grads = side_layer.astype(jnp.float32) + grad_above.astype(jnp.float32)

        def per_sequence(pair):
            return section_backward(pair[0], pair[1], w_lowrank, w_step, w_proj, rate_table, biases, gain_vector)
        outputs = lax.map(per_sequence, (x_layer, grads))
        grad_in, lowrank, dpre_half, dlow_half, dsel_half, rate_part, bias_part, skip_part = outputs
        x_replica = per_replica(x_layer)
        part_low = jnp.einsum('mdlc,mdlr->dcr', x_replica, per_replica(dlow_half))
        part_step = jnp.einsum('mdlr,mdlc->drc', per_replica(lowrank), per_replica(dpre_half))
        part_proj = jnp.einsum('mdlk,mdlc->dkc', per_replica(dsel_half), x_replica)
        part_rate = lax.optimization_barrier(jnp.sum(per_replica(rate_part), axis=0))
        part_bias = lax.optimization_barrier(jnp.sum(per_replica(bias_part), axis=0))
        part_skip = lax.optimization_barrier(jnp.sum(per_replica(skip_part), axis=0))
        summed = (combine_replicas(part_low), combine_replicas(part_step), combine_replicas(part_proj), combine_replicas(part_rate), combine_replicas(part_bias), combine_replicas(part_skip))
        return (grad_in, (grad_in,) + summed)
    packed = (by_layer(x_saved), by_layer(side_grad), w_low.reshape(LAYERS, CH, RANK), lead(w_delta, RANK), lead(w_select, 2 * NST), lead(decay_rate, NST), delta_bias.reshape(LAYERS, CH), skip_gain.reshape(LAYERS, CH))
    start = jnp.zeros((MB * N_DP, LEN, CH), jnp.bfloat16)
    _, stacked = lax.scan(one_section, start, packed, reverse=True)
    grad_stack = stacked[0].reshape(LAYERS, MB, N_DP, LEN, CH)
    ordered = jnp.take(grad_stack, plan.astype(jnp.int32), axis=1)
    grad_inputs = ordered.transpose(1, 2, 3, 0, 4).reshape(MB, N_DP * LEN, LAYERS * CH)
    grad_low = stacked[1].reshape(LAYERS * CH, RANK)
    return (grad_inputs, grad_low, unlead(stacked[2]), unlead(stacked[3]), unlead(stacked[4]), stacked[5].reshape(LAYERS * CH), stacked[6].reshape(LAYERS * CH))
```

```python
import functools

import jax
import jax.numpy as jnp
import numpy as np
from jax import lax
from jax.experimental import pallas as pl
from jax.experimental.pallas import tpu as pltpu
from jax.sharding import Mesh
from jax.sharding import PartitionSpec as P

F32, BF16 = jnp.float32, jnp.bfloat16
LAYERS = 2
WIDTH = 640
NN = (((1,), (0,)), ((), ()))
NT = (((1,), (1,)), ((), ()))
TN = (((0,), (0,)), ((), ()))
NEAR = ("yl", "x")
BOTH = ("ly", "yl", "x")
REPLICAS = ("zl", "core")
VMEM_LIMIT = 48 * 1024 * 1024


def dot(a, b, dims=NN):
    return lax.dot_general(a, b, dims, preferred_element_type=F32)


def iota(shape, dim):
    return lax.broadcasted_iota(jnp.int32, shape, dim)


def one_hot(mask):
    return jnp.where(mask, 1.0, 0.0).astype(BF16)


def spread_matrix(micro, length):
    shape = (2 * micro * length, micro * length)
    r, c = iota(shape, 0), iota(shape, 1)
    return one_hot((r % micro) * length + r // (2 * micro) == c)


def gather_matrix(micro, length, order=None):
    shape = (micro * length, 2 * micro * length)
    r, c = iota(shape, 0), iota(shape, 1)
    which = r // length
    if order is not None:
        slot, which = which, jnp.zeros(shape, jnp.int32)
        for j in range(micro):
            which = jnp.where(slot == j, order[j], which)
    return one_hot(which * length + r % length == (c % micro) * length + c // (2 * micro))


def first_half(rows, micro, lanes=128):
    return (iota((rows, lanes), 0) // micro) % 2 == 0


def pick_half(half, wide):
    return jnp.where(half, wide[:, :128], wide[:, 128:])


def two_halves(half, value):
    return jnp.concatenate([jnp.where(half, value, 0.0), jnp.where(half, 0.0, value)], axis=1)


def two_terms(value):
    high = value.astype(BF16)
    return high, (value - high.astype(F32)).astype(BF16)


def project_kernel(x_ref, wl_ref, ws_ref, out_ref):
    rank, doubled = wl_ref.shape[1], ws_ref.shape[0]
    x = x_ref[...]
    out_ref[:, :rank] = dot(x, wl_ref[...]).astype(BF16)
    out_ref[:, rank:] = jnp.zeros((x.shape[0], WIDTH - rank), BF16)
    out_ref[:, rank:rank + doubled] = dot(x, ws_ref[...], NT).astype(BF16)


def tick_kernel(micro, length, states, rank, from_above, *refs):
    x_ref, side_ref, cat_ref, wd_ref, rate_ref, bias_ref, skip_ref, *refs = refs
    if from_above:
        up_cat_ref, up_core_ref, up_low_ref, up_sel_ref, *refs = refs
        send_ref, core_ref, dpre_ref, rate_out, bias_out, skip_out, *refs = refs
    else:
        send_ref, core_ref, *refs = refs
    A, H, Bv, Cv, R, D, DX, X, G, SG, DP = refs
    rows = 2 * micro * length
    doubled = 2 * states
    half = first_half(rows, micro)
    T = spread_matrix(micro, length)
    slabs = (length, 2 * micro, 128)

    def tile(row):
        return pick_half(first_half(2 * micro, micro), row)

    x8 = pick_half(half, dot(T, x_ref[...])).reshape(slabs)
    g8 = pick_half(half, dot(T, side_ref[...]))
    if from_above:
        up = dot(T, up_cat_ref[...]).astype(BF16)
        wide = dot(up[:, :rank], up_low_ref[...], NT) + dot(up[:, rank:rank + doubled], up_sel_ref[...])
        incoming = up_core_ref[...].reshape(rows, 128) + pick_half(half, wide)
        g8 = g8 + incoming.astype(BF16).astype(F32)
    cat8 = dot(T, cat_ref[...]).astype(BF16)
    pre8 = pick_half(half, dot(cat8[:, :rank], wd_ref[...])).reshape(slabs) + tile(bias_ref[...])[None]
    step8 = jax.nn.softplus(pre8)
    X[...] = x8
    G[...] = g8.reshape(slabs)
    D[...] = step8
    DX[...] = step8 * x8
    SG[...] = jax.nn.sigmoid(pre8)
    for n in range(states):
        R[n] = tile(rate_ref[n:n + 1, :])
    wide_shape = (2 * doubled, states * 128)
    lane, row = iota(wide_shape, 1) // 128, iota(wide_shape, 0) % doubled
    terms = cat8[:, rank:rank + 2 * doubled]
    Bv[...] = dot(terms, one_hot(lane == row)).reshape(length, 2 * micro, states * 128)
    Cv[...] = dot(terms, one_hot(lane + states == row)).reshape(length, 2 * micro, states * 128)

    zero = jnp.zeros((2 * micro, 128), F32)
    for n in range(states):
        H[0, n] = zero

    def forward(t, h):
        d, dx = D[t], DX[t]
        out = []
        for n in range(states):
            a = jnp.exp(-(d * R[n]))
            h_n = a * h[n] + dx * Bv[t, :, n * 128:(n + 1) * 128]
            A[t, n] = a
            H[t + 1, n] = h_n
            out.append(h_n)
        return tuple(out)

    lax.fori_loop(0, length, forward, (zero,) * states)
    skip8 = tile(skip_ref[...])

    def backward(i, carry):
        later, acc, bias_acc, skip_acc = carry
        t = length - 1 - i
        d, dx, g, xv = D[t], DX[t], G[t], X[t]
        u, w = [zero, zero], [zero, zero]
        passed, sums = [], []
        for n in range(states):
            at = slice(n * 128, (n + 1) * 128)
            lam = Cv[t, :, at] * g + later[n]
            u[n % 2] = u[n % 2] + lam * Bv[t, :, at]
            Cv[t, :, at] = g * H[t + 1, n]
            Bv[t, :, at] = lam * dx
            back = A[t, n] * lam
            q = back * H[t, n]
            w[n % 2] = w[n % 2] + q * R[n]
            passed.append(back)
            if from_above:
                sums.append(acc[n] + d * q)
        u, w = u[0] + u[1], w[0] + w[1]
        dpre = (u * xv - w) * SG[t]
        DP[t] = dpre
        core_ref[t] = g + (u * d + skip8 * g)
        return tuple(passed), tuple(sums), bias_acc + dpre, skip_acc + g * xv

    start = ((zero,) * states, (zero,) * (states if from_above else 0), zero, zero)
    _, acc, bias_acc, skip_acc = lax.fori_loop(0, length, backward, start)

    S = gather_matrix(micro, length)
    dpre_half = dot(S, two_halves(half, DP[...].reshape(rows, 128)).astype(BF16)).astype(BF16)
    if from_above:
        lower = first_half(2 * micro, micro)
        for n in range(states):
            rate_out[n:n + 1, :] = -jnp.sum(two_halves(lower, acc[n]), axis=0, keepdims=True)
        bias_out[...] = jnp.sum(two_halves(lower, bias_acc), axis=0, keepdims=True)
        skip_out[...] = jnp.sum(two_halves(lower, skip_acc), axis=0, keepdims=True)
        dpre_ref[...] = dpre_half
    send_ref[:, :rank] = dot(dpre_half, wd_ref[...], NT).astype(BF16)
    sum_shape = (states * 128, doubled)
    depth, place = iota(sum_shape, 0) // 128, iota(sum_shape, 1)
    b_flat = Bv[...].reshape(rows, states * 128).astype(BF16)
    c_flat = Cv[...].reshape(rows, states * 128).astype(BF16)
    ds8 = dot(b_flat, one_hot(depth == place)) + dot(c_flat, one_hot(depth + states == place))
    high, low = two_terms(ds8)
    send_ref[:, rank:] = jnp.zeros((micro * length, WIDTH - rank), BF16)
    send_ref[:, rank:rank + doubled] = (dot(S, high) + dot(S, low)).astype(BF16)


def finish_kernel(micro, length, states, rank, replicas,
                  plan_ref, cat_ref, low_ref, x_ref, wl_ref, ws_ref, dpre_ref, core_ref, rate_ref, bias_ref, skip_ref,
                  grad_ref, send_ref, small):
    rows = 2 * micro * length
    doubled = 2 * states
    channels = x_ref.shape[1]
    half = first_half(rows, micro)
    T = spread_matrix(micro, length)
    cat = cat_ref[...]
    cat8 = dot(T, cat).astype(BF16)
    wide = dot(cat8[:, :rank], wl_ref[...], NT) + dot(cat8[:, rank:rank + doubled], ws_ref[...])
    grad8 = core_ref[...].reshape(rows, 128) + pick_half(half, wide)
    S = gather_matrix(micro, length, [plan_ref[j] for j in range(micro)])
    grad_ref[...] = dot(S, two_halves(half, grad8).astype(BF16)).astype(BF16)
    x = x_ref[...]
    own = channels // replicas
    part_low = dot(x, cat[:, :rank], TN).astype(BF16)
    send_ref[:, :own, :] = part_low.reshape(replicas, own, rank)
    part_delta = dot(low_ref[:, :rank], dpre_ref[...], TN).astype(BF16)
    part_delta = part_delta.reshape(replicas, rank // replicas, channels)
    deep = rank // replicas // 2
    send_ref[:, own:own + deep, :channels] = part_delta[:, :deep]
    send_ref[:, own:own + deep, channels:] = part_delta[:, deep:]
    part_sel = dot(cat[:, rank:rank + doubled], x, TN)
    small[...] = jnp.zeros(small.shape, F32)
    ds, dr = doubled // replicas, states // replicas
    for r in range(replicas):
        small[r, 0:ds, 0:channels] = part_sel[r * ds:(r + 1) * ds, :]
        small[r, 0:dr, channels:] = rate_ref[r * dr:(r + 1) * dr, :]
        small[r, dr:dr + 1, channels:channels + own] = bias_ref[:, r * own:(r + 1) * own]
        small[r, dr + 1:dr + 2, channels:channels + own] = skip_ref[:, r * own:(r + 1) * own]
    send_ref[:, own + deep:, :] = small[...].astype(BF16)


def total_kernel(got_ref, low_ref, delta_ref, sel_ref, rate_ref, bias_ref, skip_ref):
    total = got_ref[0].astype(F32)
    for r in range(1, got_ref.shape[0]):
        total = total + got_ref[r].astype(F32)
    own, channels = low_ref.shape[0], delta_ref.shape[1]
    deep = delta_ref.shape[0] // 2
    low_ref[...] = total[:own]
    delta_ref[:deep] = total[own:own + deep, :channels]
    delta_ref[deep:] = total[own:own + deep, channels:]
    rest = total[own + deep:]
    ds, dr = sel_ref.shape[0], rate_ref.shape[0]
    sel_ref[...] = rest[:ds, :channels]
    rate_ref[...] = rest[:dr, channels:]
    bias_ref[...] = rest[dr:dr + 1, channels:channels + own]
    skip_ref[...] = rest[dr + 1:dr + 2, channels:channels + own]


def call(kernel, outs, scratch, *args, scalars=0):
    vmem = pl.BlockSpec(memory_space=pltpu.VMEM)
    smem = pl.BlockSpec(memory_space=pltpu.SMEM)
    return pl.pallas_call(
        kernel,
        out_shape=[jax.ShapeDtypeStruct(*out) for out in outs],
        in_specs=[smem] * scalars + [vmem] * (len(args) - scalars),
        out_specs=[vmem] * len(outs),
        scratch_shapes=[pltpu.VMEM(shape, F32) for shape in scratch],
        compiler_params=pltpu.CompilerParams(vmem_limit_bytes=VMEM_LIMIT),
    )(*args)


def exchange(blocks, axes):
    return lax.all_to_all(blocks, axes, 0, 0)


def to_all(block, axes):
    count = lax.axis_size(axes)
    return exchange(jnp.broadcast_to(block[None], (count,) + block.shape), axes)


def total(blocks):
    return jnp.sum(blocks.astype(F32), axis=0)


def scattered_sum(rows, axes, first=0):
    count = lax.axis_size(axes)
    got = exchange(rows.reshape(count, rows.shape[0] // count, rows.shape[1]), axes)
    return total(to_all(total(got[first:]).astype(BF16), "zh"))


def per_device(x_saved, side_grad, plan, w_low, w_delta, w_select, decay_rate, delta_bias, skip_gain):
    micro, length, channels = x_saved.shape
    tokens = micro * length
    rank, doubled, states = w_low.shape[1], w_select.shape[0], decay_rate.shape[0]
    replicas = lax.axis_size(REPLICAS)
    x = x_saved.reshape(tokens, channels)
    side = side_grad.reshape(tokens, channels)
    bias, skip = delta_bias.reshape(1, channels), skip_gain.reshape(1, channels)
    down = [(1, 0)]

    part = call(project_kernel, [((tokens, WIDTH), BF16)], [], x, w_low, w_select)[0]
    up_low = lax.ppermute(w_low, "ly", down)
    up_sel = lax.ppermute(w_select, "ly", down)
    summed = scattered_sum(part, NEAR)
    selected = summed[:, rank:rank + doubled]
    high = lax.reduce_precision(selected, 8, 7)
    rest = jnp.zeros((summed.shape[0], WIDTH - rank - 2 * doubled), F32)
    packed = jnp.concatenate([summed[:, :rank], high, selected - high, rest], axis=1).astype(BF16)
    cat = to_all(packed, NEAR).reshape(tokens, WIDTH)

    slabs = (length, 2 * micro, 128)
    wide = (length, 2 * micro, states * 128)
    scratch = [(length, states, 2 * micro, 128), (length + 1, states, 2 * micro, 128), wide, wide,
               (states, 2 * micro, 128)] + [slabs] * 6
    shared = (x, side, cat, w_delta, decay_rate, bias, skip)
    send, core = call(
        functools.partial(tick_kernel, micro, length, states, rank, False),
        [((tokens, WIDTH), BF16), (slabs, F32)], scratch, *shared)
    up_core = lax.ppermute(core, "ly", down)
    upper = lax.axis_size(BOTH) // LAYERS
    up_cat = to_all(scattered_sum(send, BOTH, upper).astype(BF16), BOTH).reshape(tokens, WIDTH)

    send, core, dpre, rate_part, bias_part, skip_part = call(
        functools.partial(tick_kernel, micro, length, states, rank, True),
        [((tokens, WIDTH), BF16), (slabs, F32), ((tokens, channels), BF16), ((states, channels), F32),
         ((1, channels), F32), ((1, channels), F32)],
        scratch, *shared, up_cat, up_core, up_low, up_sel)
    down_cat = to_all(scattered_sum(send, NEAR).astype(BF16), NEAR).reshape(tokens, WIDTH)

    own, deep = channels // replicas, rank // replicas
    packed_rows = own + deep // 2 + 16
    grad, partials = call(
        functools.partial(finish_kernel, micro, length, states, rank, replicas),
        [((tokens, channels), BF16), ((replicas, packed_rows, rank), BF16)],
        [(replicas, 16, rank)],
        plan, down_cat, cat, x, w_low, w_select, dpre, core, rate_part, bias_part, skip_part, scalars=1)
    got = exchange(partials, REPLICAS)
    sums = call(
        total_kernel,
        [((own, rank), F32), ((deep, channels), F32), ((doubled // replicas, channels), F32),
         ((states // replicas, channels), F32), ((1, own), F32), ((1, own), F32)], [], got)
    return (grad.reshape(micro, length, channels), *sums[:4], sums[4].reshape(own), sums[5].reshape(own))


def solution(mesh):
    axes = ("ly", "yl", "zh", "x") + REPLICAS
    fine = Mesh(np.asarray(mesh.devices).reshape(2, 2, 4, 4, 4, 2), axes)
    section, dp = axes[:4], REPLICAS
    in_specs = (
        P(None, dp, section),
        P(None, dp, section),
        P(),
        P(section, None),
        P(None, section),
        P(None, section),
        P(None, section),
        P(section),
        P(section),
    )
    out_specs = (
        P(None, dp, section),
        P(section + dp, None),
        P(dp, section),
        P(dp, section),
        P(dp, section),
        P(section + dp),
        P(section + dp),
    )
    return jax.shard_map(per_device, mesh=fine, in_specs=in_specs, out_specs=out_specs, check_vma=False)
```

```python
import functools

import jax
import jax.numpy as jnp
import numpy as np
from jax import lax
from jax.experimental import pallas as pl
from jax.experimental.pallas import tpu as pltpu
from jax.sharding import Mesh
from jax.sharding import PartitionSpec as P

F32, BF16 = jnp.float32, jnp.bfloat16
WIDTH = 640
NN = (((1,), (0,)), ((), ()))
NT = (((1,), (1,)), ((), ()))
TN = (((0,), (0,)), ((), ()))
NEAR = ("yl", "x")
REPLICAS = ("zl", "core")
VMEM_LIMIT = 48 * 1024 * 1024
PROJECT_LIMIT = 60 * 1024 * 1024
SEL_ROWS = 8
UNROLL = 1


def dot(a, b, dims=NN):
    return lax.dot_general(a, b, dims, preferred_element_type=F32)


def iota(shape, dim):
    return lax.broadcasted_iota(jnp.int32, shape, dim)


def one_hot(mask):
    return jnp.where(mask, 1.0, 0.0).astype(BF16)


def spread_matrix(micro, length):
    shape = (2 * micro * length, micro * length)
    r, c = iota(shape, 0), iota(shape, 1)
    return one_hot((r % micro) * length + r // (2 * micro) == c)


def gather_matrix(micro, length, order=None):
    shape = (micro * length, 2 * micro * length)
    r, c = iota(shape, 0), iota(shape, 1)
    which = r // length
    if order is not None:
        slot, which = which, jnp.zeros(shape, jnp.int32)
        for j in range(micro):
            which = jnp.where(slot == j, order[j], which)
    return one_hot(which * length + r % length == (c % micro) * length + c // (2 * micro))


def first_half(rows, micro, lanes=128):
    return (iota((rows, lanes), 0) // micro) % 2 == 0


def pick_half(half, wide):
    return jnp.where(half, wide[:, :128], wide[:, 128:])


def two_halves(half, value):
    return jnp.concatenate([jnp.where(half, value, 0.0), jnp.where(half, 0.0, value)], axis=1)


def two_terms(value):
    high = value.astype(BF16)
    return high, (value - high.astype(F32)).astype(BF16)


def fetch(sources, targets, sems):
    copies = [pltpu.make_async_copy(src, dst, sems.at[i]) for i, (src, dst) in enumerate(zip(sources, targets))]
    for copy in copies:
        copy.start()
    return copies


def project_kernel(x_hbm, ws_hbm, wl_hbm, rate_hbm, bias_hbm, skip_hbm, out_ref, const_ref,
                   x_ref, ws_ref, wl_ref, rate_ref, bias_ref, skip_ref, sems):
    copies = fetch((x_hbm, wl_hbm, ws_hbm, rate_hbm, bias_hbm, skip_hbm),
                   (x_ref, wl_ref, ws_ref, rate_ref, bias_ref, skip_ref), sems)
    rank, doubled, states = wl_ref.shape[1], ws_ref.shape[0], rate_ref.shape[0]
    const_ref[...] = jnp.zeros(const_ref.shape, F32)
    out_ref[:, rank:] = jnp.zeros((x_ref.shape[0], WIDTH - rank), BF16)
    for copy in copies:
        copy.wait()
    x = x_ref[...]
    out_ref[:, :rank] = dot(x, wl_ref[...]).astype(BF16)
    out_ref[:, rank:rank + doubled] = dot(x, ws_ref[...], NT).astype(BF16)
    const_ref[:states, :] = rate_ref[...]
    const_ref[states:states + 1, :] = bias_ref[...]
    const_ref[states + 1:states + 2, :] = skip_ref[...]


def forward(micro, length, states, rank, x, cat, wd, const_ref, A, H, Bv, Cv, R, X, D, DX, SG):
    rows = 2 * micro * length
    doubled = 2 * states
    half = first_half(rows, micro)
    lower = first_half(2 * micro, micro)
    T = spread_matrix(micro, length)
    slabs = (length, 2 * micro, 128)
    cat8 = dot(T, cat).astype(BF16)
    x8 = pick_half(half, dot(T, x)).reshape(slabs)
    wide_shape = (2 * doubled, states * 128)
    lane, row = iota(wide_shape, 1) // 128, iota(wide_shape, 0) % doubled
    terms = cat8[:, rank:rank + 2 * doubled]
    Bv[...] = dot(terms, one_hot(lane == row)).reshape(length, 2 * micro, states * 128)
    Cv[...] = dot(terms, one_hot(lane + states == row)).reshape(length, 2 * micro, states * 128)
    pre8 = pick_half(half, dot(cat8[:, :rank], wd)).reshape(slabs)
    pre8 = pre8 + pick_half(lower, const_ref[states:states + 1, :])[None]
    step8 = jax.nn.softplus(pre8)
    X[...] = x8
    D[...] = step8
    DX[...] = step8 * x8
    SG[...] = jax.nn.sigmoid(pre8)
    zero = jnp.zeros((2 * micro, 128), F32)
    for n in range(states):
        R[n] = pick_half(lower, const_ref[n:n + 1, :])
        H[0, n] = zero

    def ahead(t, h):
        d, dx = D[t], DX[t]
        out = []
        for n in range(states):
            a = jnp.exp(-(d * R[n]))
            h_n = a * h[n] + dx * Bv[t, :, n * 128:(n + 1) * 128]
            A[t, n] = a
            H[t + 1, n] = h_n
            out.append(h_n)
        return tuple(out)

    lax.fori_loop(0, length, ahead, (zero,) * states, unroll=UNROLL)


def backward(micro, length, states, rank, sums, wd, const_ref, G, A, H, Bv, Cv, R, X, D, DX, SG,
             send_ref, core_ref, Pb, Pc, DP):
    rows = 2 * micro * length
    doubled = 2 * states
    half = first_half(rows, micro)
    zero = jnp.zeros((2 * micro, 128), F32)
    skip8 = pick_half(first_half(2 * micro, micro), const_ref[states + 1:states + 2, :])

    def back(i, carry):
        later, acc, bias_acc, skip_acc = carry
        t = length - 1 - i
        d, dx, g, xv = D[t], DX[t], G[t], X[t]
        u, w = [zero, zero], [zero, zero]
        passed, added = [], []
        for n in range(states):
            at = slice(n * 128, (n + 1) * 128)
            lam = Cv[t, :, at] * g + later[n]
            u[n % 2] = u[n % 2] + lam * Bv[t, :, at]
            Pc[t, :, at] = g * H[t + 1, n]
            Pb[t, :, at] = lam * dx
            through = A[t, n] * lam
            q = through * H[t, n]
            w[n % 2] = w[n % 2] + q * R[n]
            passed.append(through)
            if sums:
                added.append(acc[n] + d * q)
        u, w = u[0] + u[1], w[0] + w[1]
        dpre = (u * xv - w) * SG[t]
        DP[t] = dpre
        core_ref[t] = g + (u * d + skip8 * g)
        if sums:
            bias_acc, skip_acc = bias_acc + dpre, skip_acc + g * xv
        return tuple(passed), tuple(added), bias_acc, skip_acc

    start = ((zero,) * states, (zero,) * (states if sums else 0), zero, zero)
    _, acc, bias_acc, skip_acc = lax.fori_loop(0, length, back, start, unroll=UNROLL)
    S = gather_matrix(micro, length)
    dpre_half = dot(S, two_halves(half, DP[...].reshape(rows, 128)).astype(BF16)).astype(BF16)
    send_ref[:, :rank] = dot(dpre_half, wd, NT).astype(BF16)
    sum_shape = (states * 128, doubled)
    depth, place = iota(sum_shape, 0) // 128, iota(sum_shape, 1)
    b_flat = Pb[...].reshape(rows, states * 128).astype(BF16)
    c_flat = Pc[...].reshape(rows, states * 128).astype(BF16)
    ds8 = dot(b_flat, one_hot(depth == place)) + dot(c_flat, one_hot(depth + states == place))
    high, low = two_terms(ds8)
    send_ref[:, rank:] = jnp.zeros((micro * length, WIDTH - rank), BF16)
    send_ref[:, rank:rank + doubled] = (dot(S, high) + dot(S, low)).astype(BF16)
    return dpre_half, acc, bias_acc, skip_acc


def tick_kernel(micro, length, states, rank, from_above, *refs):
    x_ref, side_ref, cat_ref, wd_ref, const_ref, *refs = refs
    if from_above:
        above_ref, send_ref, core_ref, dpre_ref, rate_out, ends_ref, *refs = refs
    else:
        send_ref, core_ref, *refs = refs
    G, Pb, Pc, DP, *state = refs
    rows = 2 * micro * length
    channels = x_ref.shape[1]
    half = first_half(rows, micro)
    T = spread_matrix(micro, length)
    g8 = pick_half(half, dot(T, side_ref[...]))
    if from_above:
        g8 = g8 + pick_half(half, dot(T, above_ref[...]))
    G[...] = g8.reshape(G.shape)
    forward(micro, length, states, rank, x_ref[...], cat_ref[...], wd_ref[...], const_ref, *state)
    dpre_half, acc, bias_acc, skip_acc = backward(
        micro, length, states, rank, from_above, wd_ref[...], const_ref, G, *state, send_ref, core_ref, Pb, Pc, DP)
    if from_above:
        dpre_ref[...] = dpre_half
        for n in range(states):
            rate_out[n] = acc[n]
        ends_ref[0] = bias_acc
        ends_ref[1] = skip_acc


def layer_grad(micro, length, states, rank, cat_ref, wl_ref, ws_ref, core_ref):
    rows = 2 * micro * length
    half = first_half(rows, micro)
    cat8 = dot(spread_matrix(micro, length), cat_ref[...]).astype(BF16)
    wide = dot(cat8[:, :rank], wl_ref[...], NT) + dot(cat8[:, rank:rank + 2 * states], ws_ref[...])
    return two_halves(half, core_ref[...].reshape(rows, 128) + pick_half(half, wide)).astype(BF16)


def hand_kernel(micro, length, states, rank, cat_ref, wl_ref, ws_ref, core_ref, grad_ref):
    grad8 = layer_grad(micro, length, states, rank, cat_ref, wl_ref, ws_ref, core_ref)
    grad_ref[...] = dot(gather_matrix(micro, length), grad8).astype(BF16)


def order_kernel(micro, length, states, rank, plan_hbm, cat_ref, wl_ref, ws_ref, core_ref, grad_ref, plan_ref, sems):
    copies = fetch((plan_hbm,), (plan_ref,), sems)
    grad8 = layer_grad(micro, length, states, rank, cat_ref, wl_ref, ws_ref, core_ref)
    copies[0].wait()
    S = gather_matrix(micro, length, [plan_ref[j] for j in range(micro)])
    grad_ref[...] = dot(S, grad8).astype(BF16)


def part_kernel(micro, replicas, cat_ref, down_ref, x_ref, dpre_ref, rate_ref, ends_ref, send_ref, small):
    states = rate_ref.shape[0]
    channels, rank = x_ref.shape[1], (send_ref.shape[2] - 128) // 2
    own, deep, doubled = channels // replicas, rank // replicas, 2 * states
    share, rate_share = doubled // replicas, states // replicas
    x, down = x_ref[...], down_ref[...]
    send_ref[:, :, :rank] = dot(x, down[:, :rank], TN).astype(BF16).reshape(replicas, own, rank)
    delta = dot(cat_ref[:, :rank], dpre_ref[...], TN).astype(BF16).reshape(replicas, deep, channels)
    send_ref[:, :, rank:rank + channels] = delta[:, :own]
    send_ref[:, :, rank + channels:2 * rank] = delta[:, own:]
    select = dot(down[:, rank:rank + doubled], x, TN)
    lower = first_half(2 * micro, micro)

    def row_of(value):
        return jnp.sum(two_halves(lower, value), axis=0, keepdims=True)

    small[...] = jnp.zeros(small.shape, F32)
    for r in range(replicas):
        for k in range(2):
            small[r, k * share:(k + 1) * share, :] = select[r * share:(r + 1) * share, k * 128:(k + 1) * 128]
    for n in range(states):
        row = -row_of(rate_ref[n])
        at = SEL_ROWS + 2 * (n % rate_share)
        small[n // rate_share, at:at + 1, :] = row[:, :128]
        small[n // rate_share, at + 1:at + 2, :] = row[:, 128:]
    at = SEL_ROWS + 2 * rate_share
    for k in range(2):
        row = row_of(ends_ref[k])
        for r in range(replicas):
            small[r, at + k:at + k + 1, :own] = row[:, r * own:(r + 1) * own]
    send_ref[:, :, 2 * rank:] = small[...].astype(BF16)


def total_kernel(got_ref, low_ref, delta_ref, sel_ref, rate_ref, bias_ref, skip_ref):
    own, rank = low_ref.shape
    channels = delta_ref.shape[1]

    def summed(lanes):
        value = got_ref[0, :, lanes].astype(F32)
        for r in range(1, got_ref.shape[0]):
            value = value + got_ref[r, :, lanes].astype(F32)
        return value

    low_ref[...] = summed(slice(0, rank))
    delta_ref[:own] = summed(slice(rank, rank + channels))
    delta_ref[own:] = summed(slice(rank + channels, 2 * rank))
    small = summed(slice(2 * rank, 2 * rank + 128))
    rows, share = sel_ref.shape[0], rate_ref.shape[0]
    for k in range(2):
        sel_ref[:, k * 128:(k + 1) * 128] = small[k * rows:(k + 1) * rows]
        for n in range(share):
            at = SEL_ROWS + 2 * n + k
            rate_ref[n:n + 1, k * 128:(k + 1) * 128] = small[at:at + 1]
    at = SEL_ROWS + 2 * share
    bias_ref[...] = small[at:at + 1, :own]
    skip_ref[...] = small[at + 1:at + 2, :own]


def call(kernel, outs, scratch, *args, far=0, limit=VMEM_LIMIT):
    vmem = pl.BlockSpec(memory_space=pltpu.VMEM)
    hbm = pl.BlockSpec(memory_space=pl.ANY)
    return pl.pallas_call(
        kernel,
        out_shape=[jax.ShapeDtypeStruct(*out) for out in outs],
        in_specs=[hbm] * far + [vmem] * (len(args) - far),
        out_specs=[vmem] * len(outs),
        scratch_shapes=[pltpu.VMEM(s, F32) if isinstance(s, tuple) else s for s in scratch],
        compiler_params=pltpu.CompilerParams(vmem_limit_bytes=limit),
    )(*args)


def exchange(blocks, axes):
    return lax.all_to_all(blocks, axes, 0, 0)


def to_all(block, axes):
    count = lax.axis_size(axes)
    return exchange(jnp.broadcast_to(block[None], (count,) + block.shape), axes)


def total(blocks):
    return jnp.sum(blocks.astype(F32), axis=0)


def scattered_sum(rows, axes):
    count = lax.axis_size(axes)
    got = exchange(rows.reshape(count, rows.shape[0] // count, rows.shape[1]), axes)
    return total(to_all(total(got).astype(BF16), "zh"))


def per_device(x_saved, side_grad, plan, w_low, w_delta, w_select, decay_rate, delta_bias, skip_gain):
    micro, length, channels = x_saved.shape
    tokens = micro * length
    rank, doubled, states = w_low.shape[1], w_select.shape[0], decay_rate.shape[0]
    replicas = lax.axis_size(REPLICAS)
    x = x_saved.reshape(tokens, channels)
    side = side_grad.reshape(tokens, channels)
    bias, skip = delta_bias.reshape(1, channels), skip_gain.reshape(1, channels)

    sources = (x, w_select, w_low, decay_rate, bias, skip)
    part, const = call(
        project_kernel, [((tokens, WIDTH), BF16), ((states + 8, channels), F32)],
        [pltpu.VMEM(a.shape, a.dtype) for a in sources] + [pltpu.SemaphoreType.DMA((len(sources),))],
        *sources, far=len(sources), limit=PROJECT_LIMIT)
    summed = scattered_sum(part, NEAR)
    selected = summed[:, rank:rank + doubled]
    high = lax.reduce_precision(selected, 8, 7)
    rest = summed[:, rank + 2 * doubled:]
    packed = jnp.concatenate([summed[:, :rank], high, selected - high, rest], axis=1).astype(BF16)
    cat = to_all(packed, NEAR).reshape(tokens, WIDTH)

    dims = (micro, length, states, rank)
    slab, flat = (length, 2 * micro, 128), (length, 2 * micro, states * 128)
    send_out = ((tokens, WIDTH), BF16)
    scratch = [slab, flat, flat, slab, (length, states, 2 * micro, 128), (length + 1, states, 2 * micro, 128),
               flat, flat, (states, 2 * micro, 128), slab, slab, slab, slab]
    shared = (x, side, cat, w_delta, const)
    send, core = call(
        functools.partial(tick_kernel, *dims, False), [send_out, (slab, F32)], scratch, *shared)
    cat_up = to_all(scattered_sum(send, NEAR).astype(BF16), NEAR).reshape(tokens, WIDTH)
    handed, = call(
        functools.partial(hand_kernel, *dims), [((tokens, channels), BF16)], [], cat_up, w_low, w_select, core)
    above = lax.ppermute(handed, "ly", [(1, 0)])

    send, core, dpre, rate_sum, end_sums = call(
        functools.partial(tick_kernel, *dims, True),
        [send_out, (slab, F32), ((tokens, channels), BF16), ((states, 2 * micro, 128), F32),
         ((2, 2 * micro, 128), F32)], scratch, *shared, above)
    down_cat = to_all(scattered_sum(send, NEAR).astype(BF16), NEAR).reshape(tokens, WIDTH)

    own = channels // replicas
    partials, = call(
        functools.partial(part_kernel, micro, replicas), [((replicas, own, 2 * rank + 128), BF16)],
        [(replicas, own, 128)], cat, down_cat, x, dpre, rate_sum, end_sums)
    got = exchange(partials, REPLICAS)
    grad, = call(
        functools.partial(order_kernel, *dims), [((tokens, channels), BF16)],
        [pltpu.SMEM((micro,), jnp.int32), pltpu.SemaphoreType.DMA((1,))],
        plan, down_cat, w_low, w_select, core, far=1)
    sums = call(
        total_kernel,
        [((own, rank), F32), ((rank // replicas, channels), F32), ((doubled // replicas, channels), F32),
         ((states // replicas, channels), F32), ((1, own), F32), ((1, own), F32)], [], got)
    return (grad.reshape(micro, length, channels), *sums[:4], sums[4].reshape(own), sums[5].reshape(own))


def solution(mesh):
    axes = ("ly", "yl", "zh", "x") + REPLICAS
    fine = Mesh(np.asarray(mesh.devices).reshape(2, 2, 4, 4, 4, 2), axes)
    section, dp = axes[:4], REPLICAS
    in_specs = (
        P(None, dp, section),
        P(None, dp, section),
        P(),
        P(section, None),
        P(None, section),
        P(None, section),
        P(None, section),
        P(section),
        P(section),
    )
    out_specs = (
        P(None, dp, section),
        P(section + dp, None),
        P(dp, section),
        P(dp, section),
        P(dp, section),
        P(section + dp),
        P(section + dp),
    )
    return jax.shard_map(per_device, mesh=fine, in_specs=in_specs, out_specs=out_specs, check_vma=False)
```

```python
import functools

import jax
import jax.numpy as jnp
import numpy as np
from jax import lax
from jax.experimental import pallas as pl
from jax.experimental.pallas import tpu as pltpu
from jax.sharding import Mesh
from jax.sharding import PartitionSpec as P

F32, BF16 = jnp.float32, jnp.bfloat16
WIDTH = 640
NN = (((1,), (0,)), ((), ()))
NT = (((1,), (1,)), ((), ()))
TN = (((0,), (0,)), ((), ()))
NEAR = ("yl", "x")
REPLICAS = ("zl", "core")
VMEM_LIMIT = 48 * 1024 * 1024
PROJECT_LIMIT = 60 * 1024 * 1024
SEL_ROWS = 8
UNROLL = 32


def dot(a, b, dims=NN):
    return lax.dot_general(a, b, dims, preferred_element_type=F32)


def iota(shape, dim):
    return lax.broadcasted_iota(jnp.int32, shape, dim)


def one_hot(mask):
    return jnp.where(mask, 1.0, 0.0).astype(BF16)


def spread_matrix(micro, length):
    shape = (2 * micro * length, micro * length)
    r, c = iota(shape, 0), iota(shape, 1)
    return one_hot((r % micro) * length + r // (2 * micro) == c)


def gather_matrix(micro, length):
    shape = (micro * length, 2 * micro * length)
    r, c = iota(shape, 0), iota(shape, 1)
    return one_hot(r == (c % micro) * length + c // (2 * micro))


def first_half(rows, micro, lanes=128):
    return (iota((rows, lanes), 0) // micro) % 2 == 0


def pick_half(half, wide):
    return jnp.where(half, wide[:, :128], wide[:, 128:])


def two_halves(half, value):
    return jnp.concatenate([jnp.where(half, value, 0.0), jnp.where(half, 0.0, value)], axis=1)


def two_terms(value):
    high = value.astype(BF16)
    return high, (value - high.astype(F32)).astype(BF16)


def fetch(sources, targets, sems):
    copies = [pltpu.make_async_copy(src, dst, sems.at[i]) for i, (src, dst) in enumerate(zip(sources, targets))]
    for copy in copies:
        copy.start()
    return copies


def project_kernel(x_hbm, ws_hbm, wl_hbm, rate_hbm, bias_hbm, skip_hbm, out_ref, const_ref,
                   x_ref, ws_ref, wl_ref, rate_ref, bias_ref, skip_ref, sems):
    copies = fetch((x_hbm, wl_hbm, ws_hbm, rate_hbm, bias_hbm, skip_hbm),
                   (x_ref, wl_ref, ws_ref, rate_ref, bias_ref, skip_ref), sems)
    rank, doubled, states = wl_ref.shape[1], ws_ref.shape[0], rate_ref.shape[0]
    const_ref[...] = jnp.zeros(const_ref.shape, F32)
    out_ref[:, rank:] = jnp.zeros((x_ref.shape[0], WIDTH - rank), BF16)
    for copy in copies:
        copy.wait()
    x = x_ref[...]
    out_ref[:, :rank] = dot(x, wl_ref[...]).astype(BF16)
    out_ref[:, rank:rank + doubled] = dot(x, ws_ref[...], NT).astype(BF16)
    const_ref[:states, :] = rate_ref[...]
    const_ref[states:states + 1, :] = bias_ref[...]
    const_ref[states + 1:states + 2, :] = skip_ref[...]


def state_lanes(states):
    shape = (2 * states, 2 * states * 128)
    return one_hot(iota(shape, 1) // 128 == iota(shape, 0))


def grouped_sums(value, count, group=8):
    shape = (group * 128, group)
    ones = one_hot(iota(shape, 0) // 128 == iota(shape, 1))
    parts = [dot(value[:, at * 128:(at + group) * 128], ones) for at in range(0, count, group)]
    return jnp.concatenate(parts, axis=1)


def put_rows(ref, micro, value):
    length = value.shape[0] // micro
    for k in range(2):
        for m in range(micro):
            ref[pl.ds(k * micro + m, length, stride=2 * micro), :] = value[m * length:(m + 1) * length, k * 128:(k + 1) * 128]


def get_rows(ref, micro):
    length = ref.shape[0] // (2 * micro)
    return jnp.concatenate([jnp.concatenate(
        [ref[pl.ds(k * micro + m, length, stride=2 * micro), :] for m in range(micro)], axis=0)
        for k in range(2)], axis=1)


def forward(micro, length, states, rank, x, cat, wd, const_ref, DP, A, H, BC, R, X, D, DX, SG):
    rows = 2 * micro * length
    doubled = 2 * states
    half = first_half(rows, micro)
    lower = first_half(2 * micro, micro)
    T = spread_matrix(micro, length)
    slabs = (length, 2 * micro, 128)
    cat8 = dot(T, cat[:, rank:rank + 2 * doubled]).astype(BF16)
    x8 = pick_half(half, dot(T, x)).reshape(slabs)
    pick = state_lanes(states)
    BC[...] = dot(cat8, jnp.concatenate([pick, pick], axis=0)).reshape(BC.shape)
    put_rows(DP, micro, dot(cat[:, :rank], wd))
    pre8 = DP[...].reshape(slabs)
    pre8 = pre8 + pick_half(lower, const_ref[states:states + 1, :])[None]
    step8 = jax.nn.softplus(pre8)
    X[...] = x8
    D[...] = step8
    DX[...] = step8 * x8
    SG[...] = jax.nn.sigmoid(pre8)
    zero = jnp.zeros((2 * micro, 128), F32)
    for n in range(states):
        R[n] = pick_half(lower, const_ref[n:n + 1, :])
        H[0, n] = zero

    def ahead(t, h):
        d, dx = D[t], DX[t]
        out = []
        for n in range(states):
            a = jnp.exp(-(d * R[n]))
            h_n = a * h[n] + dx * BC[t, :, n * 128:(n + 1) * 128]
            A[t, n] = a
            H[t + 1, n] = h_n
            out.append(h_n)
        return tuple(out)

    lax.fori_loop(0, length, ahead, (zero,) * states, unroll=UNROLL)


def backward(micro, length, states, rank, sums, wd, const_ref, G, A, H, BC, R, X, D, DX, SG,
             send_ref, core_ref, products, DP, C):
    rows = 2 * micro * length
    doubled = 2 * states
    half = first_half(rows, micro)
    zero = jnp.zeros((2 * micro, 128), F32)
    skip8 = pick_half(first_half(2 * micro, micro), const_ref[states + 1:states + 2, :])

    def back(i, carry):
        later, bias_acc, skip_acc = carry
        pair = length // 2 - 1 - i
        times = (2 * pair, 2 * pair + 1)
        d, dx, g, xv = ([ref[t] for t in times] for ref in (D, DX, G, X))
        u, w = [zero, zero], [zero, zero]
        passed = []
        for n in range(states):
            rate = R[n]
            b_at, c_at = (slice(at * 128, (at + 1) * 128) for at in (n, states + n))
            h = [H[times[0] + k, n] for k in range(3)]
            lam, q = [None, None], [None, None]
            through = later[n]
            for k in (1, 0):
                lam[k] = BC[times[k], :, c_at] * g[k] + through
                through = A[times[k], n] * lam[k]
                q[k] = through * h[k]
                u[k] = u[k] + lam[k] * BC[times[k], :, b_at]
                w[k] = w[k] + q[k] * rate
            for at, value in ((b_at, [lam[k] * dx[k] for k in range(2)]),
                              (c_at, [g[k] * h[k + 1] for k in range(2)])):
                products[pair, :, at] = jnp.concatenate(value, axis=0).astype(BF16)
            passed.append(through)
            if sums is not None:
                sums[n] = sums[n] + (d[0] * q[0] + d[1] * q[1])
        for k in range(2):
            dpre = (u[k] * xv[k] - w[k]) * SG[times[k]]
            DP[pl.ds(times[k] * 2 * micro, 2 * micro), :] = dpre
            C[pl.ds(times[k] * 2 * micro, 2 * micro), :] = g[k] + (u[k] * d[k] + skip8 * g[k])
            if sums is not None:
                bias_acc, skip_acc = bias_acc + dpre, skip_acc + g[k] * xv[k]
        return tuple(passed), bias_acc, skip_acc

    if sums is not None:
        sums[...] = jnp.zeros(sums.shape, F32)
    start = ((zero,) * states, zero, zero)
    _, bias_acc, skip_acc = lax.fori_loop(0, length // 2, back, start, unroll=16)
    S = gather_matrix(micro, length)
    core_ref[...] = get_rows(C, micro)
    dpre_half = get_rows(DP, micro).astype(BF16)
    send_ref[:, :rank] = dot(dpre_half, wd, NT).astype(BF16)
    high, low = two_terms(grouped_sums(products[...].reshape(rows, doubled * 128), doubled))
    send_ref[:, rank:] = jnp.zeros((micro * length, WIDTH - rank), BF16)
    send_ref[:, rank:rank + doubled] = (dot(S, high) + dot(S, low)).astype(BF16)
    return dpre_half, bias_acc, skip_acc


def tick_kernel(micro, length, states, rank, from_above, *refs):
    x_ref, side_ref, cat_ref, wd_ref, const_ref, *refs = refs
    if from_above:
        above_ref, send_ref, core_ref, dpre_ref, rate_out, ends_ref, *refs = refs
    else:
        send_ref, core_ref, *refs = refs
    G, products, DP, C, *state = refs
    rows = 2 * micro * length
    channels = x_ref.shape[1]
    half = first_half(rows, micro)
    T = spread_matrix(micro, length)
    g8 = pick_half(half, dot(T, side_ref[...]))
    if from_above:
        g8 = g8 + pick_half(half, dot(T, above_ref[...]))
    G[...] = g8.reshape(G.shape)
    forward(micro, length, states, rank, x_ref[...], cat_ref[...], wd_ref[...], const_ref, DP, *state)
    dpre_half, bias_acc, skip_acc = backward(
        micro, length, states, rank, rate_out if from_above else None, wd_ref[...], const_ref, G, *state, send_ref, core_ref, products, DP, C)
    if from_above:
        dpre_ref[...] = dpre_half
        ends_ref[0] = bias_acc
        ends_ref[1] = skip_acc


def layer_grad(cat_ref, wl_ref, ws_ref, core_ref):
    rank, doubled = wl_ref.shape[1], ws_ref.shape[0]
    value = core_ref[...] + dot(cat_ref[:, :rank], wl_ref[...], NT)
    return (value + dot(cat_ref[:, rank:rank + doubled], ws_ref[...])).astype(BF16)


def hand_kernel(cat_ref, wl_ref, ws_ref, core_ref, grad_ref):
    grad_ref[...] = layer_grad(cat_ref, wl_ref, ws_ref, core_ref)


def order_kernel(plan_hbm, cat_ref, wl_ref, ws_ref, core_ref, grad_ref, held, plan_ref, sems):
    copies = fetch((plan_hbm,), (plan_ref,), sems)
    held[...] = layer_grad(cat_ref, wl_ref, ws_ref, core_ref).reshape(held.shape)
    copies[0].wait()
    for j in range(grad_ref.shape[0]):
        grad_ref[j] = held[plan_ref[j]]


def part_kernel(micro, replicas, cat_ref, down_ref, x_ref, dpre_ref, rate_ref, ends_ref, send_ref, small):
    states = rate_ref.shape[0]
    channels, rank = x_ref.shape[1], (send_ref.shape[2] - 128) // 2
    own, deep, doubled = channels // replicas, rank // replicas, 2 * states
    share, rate_share = doubled // replicas, states // replicas
    x, down = x_ref[...], down_ref[...]
    send_ref[:, :, :rank] = dot(x, down[:, :rank], TN).astype(BF16).reshape(replicas, own, rank)
    delta = dot(cat_ref[:, :rank], dpre_ref[...], TN).astype(BF16).reshape(replicas, deep, channels)
    send_ref[:, :, rank:rank + channels] = delta[:, :own]
    send_ref[:, :, rank + channels:2 * rank] = delta[:, own:]
    select = dot(down[:, rank:rank + doubled], x, TN)
    lower = first_half(2 * micro, micro)

    def row_of(value):
        return jnp.sum(two_halves(lower, value), axis=0, keepdims=True)

    small[...] = jnp.zeros(small.shape, F32)
    for r in range(replicas):
        for k in range(2):
            small[r, k * share:(k + 1) * share, :] = select[r * share:(r + 1) * share, k * 128:(k + 1) * 128]
    for n in range(states):
        row = -row_of(rate_ref[n])
        at = SEL_ROWS + 2 * (n % rate_share)
        small[n // rate_share, at:at + 1, :] = row[:, :128]
        small[n // rate_share, at + 1:at + 2, :] = row[:, 128:]
    at = SEL_ROWS + 2 * rate_share
    for k in range(2):
        row = row_of(ends_ref[k])
        for r in range(replicas):
            small[r, at + k:at + k + 1, :own] = row[:, r * own:(r + 1) * own]
    send_ref[:, :, 2 * rank:] = small[...].astype(BF16)


def total_kernel(got_ref, low_ref, delta_ref, sel_ref, rate_ref, bias_ref, skip_ref):
    own, rank = low_ref.shape
    channels = delta_ref.shape[1]

    def summed(lanes):
        value = got_ref[0, :, lanes].astype(F32)
        for r in range(1, got_ref.shape[0]):
            value = value + got_ref[r, :, lanes].astype(F32)
        return value

    low_ref[...] = summed(slice(0, rank))
    delta_ref[:own] = summed(slice(rank, rank + channels))
    delta_ref[own:] = summed(slice(rank + channels, 2 * rank))
    small = summed(slice(2 * rank, 2 * rank + 128))
    rows, share = sel_ref.shape[0], rate_ref.shape[0]
    for k in range(2):
        sel_ref[:, k * 128:(k + 1) * 128] = small[k * rows:(k + 1) * rows]
        for n in range(share):
            at = SEL_ROWS + 2 * n + k
            rate_ref[n:n + 1, k * 128:(k + 1) * 128] = small[at:at + 1]
    at = SEL_ROWS + 2 * share
    bias_ref[...] = small[at:at + 1, :own]
    skip_ref[...] = small[at + 1:at + 2, :own]


def call(kernel, outs, scratch, *args, far=0, limit=VMEM_LIMIT):
    vmem = pl.BlockSpec(memory_space=pltpu.VMEM)
    hbm = pl.BlockSpec(memory_space=pl.ANY)
    return pl.pallas_call(
        kernel,
        out_shape=[jax.ShapeDtypeStruct(*out) for out in outs],
        in_specs=[hbm] * far + [vmem] * (len(args) - far),
        out_specs=[vmem] * len(outs),
        scratch_shapes=[pltpu.VMEM(s, F32) if isinstance(s, tuple) else s for s in scratch],
        compiler_params=pltpu.CompilerParams(vmem_limit_bytes=limit),
    )(*args)


def exchange(blocks, axes):
    return lax.all_to_all(blocks, axes, 0, 0)


def to_all(block, axes):
    count = lax.axis_size(axes)
    return exchange(jnp.broadcast_to(block[None], (count,) + block.shape), axes)


def total(blocks):
    return jnp.sum(blocks.astype(F32), axis=0)


def scattered_sum(rows, axes):
    count = lax.axis_size(axes)
    got = exchange(rows.reshape(count, rows.shape[0] // count, rows.shape[1]), axes)
    return total(to_all(total(got).astype(BF16), "zh"))


def per_device(x_saved, side_grad, plan, w_low, w_delta, w_select, decay_rate, delta_bias, skip_gain):
    micro, length, channels = x_saved.shape
    tokens = micro * length
    rank, doubled, states = w_low.shape[1], w_select.shape[0], decay_rate.shape[0]
    replicas = lax.axis_size(REPLICAS)
    x = x_saved.reshape(tokens, channels)
    side = side_grad.reshape(tokens, channels)
    bias, skip = delta_bias.reshape(1, channels), skip_gain.reshape(1, channels)

    sources = (x, w_select, w_low, decay_rate, bias, skip)
    part, const = call(
        project_kernel, [((tokens, WIDTH), BF16), ((states + 8, channels), F32)],
        [pltpu.VMEM(a.shape, a.dtype) for a in sources] + [pltpu.SemaphoreType.DMA((len(sources),))],
        *sources, far=len(sources), limit=PROJECT_LIMIT)
    summed = scattered_sum(part, NEAR)
    selected = summed[:, rank:rank + doubled]
    high = lax.reduce_precision(selected, 8, 7)
    rest = summed[:, rank + 2 * doubled:]
    packed = jnp.concatenate([summed[:, :rank], high, selected - high, rest], axis=1).astype(BF16)
    cat = to_all(packed, NEAR).reshape(tokens, WIDTH)

    dims = (micro, length, states, rank)
    slab, rows_all = (length, 2 * micro, 128), 2 * tokens
    send_out = ((tokens, WIDTH), BF16)
    scratch = [slab, pltpu.VMEM((length // 2, 4 * micro, doubled * 128), BF16), (rows_all, 128), (rows_all, 128),
               (length, states, 2 * micro, 128), (length + 1, states, 2 * micro, 128),
               (length, 2 * micro, doubled * 128), (states, 2 * micro, 128), slab, slab, slab, slab]
    shared = (x, side, cat, w_delta, const)
    send, core = call(
        functools.partial(tick_kernel, *dims, False), [send_out, ((tokens, channels), F32)], scratch, *shared)
    cat_up = to_all(scattered_sum(send, NEAR).astype(BF16), NEAR).reshape(tokens, WIDTH)
    handed, = call(
        hand_kernel, [((tokens, channels), BF16)], [], cat_up, w_low, w_select, core)
    above = lax.ppermute(handed, "ly", [(1, 0)])

    send, core, dpre, rate_sum, end_sums = call(
        functools.partial(tick_kernel, *dims, True),
        [send_out, ((tokens, channels), F32), ((tokens, channels), BF16), ((states, 2 * micro, 128), F32),
         ((2, 2 * micro, 128), F32)], scratch, *shared, above)
    down_cat = to_all(scattered_sum(send, NEAR).astype(BF16), NEAR).reshape(tokens, WIDTH)

    own = channels // replicas
    partials, = call(
        functools.partial(part_kernel, micro, replicas), [((replicas, own, 2 * rank + 128), BF16)],
        [(replicas, own, 128)], cat, down_cat, x, dpre, rate_sum, end_sums)
    got = exchange(partials, REPLICAS)
    grad, = call(
        order_kernel, [((micro, length, channels), BF16)],
        [pltpu.VMEM((micro, length, channels), BF16), pltpu.SMEM((micro,), jnp.int32), pltpu.SemaphoreType.DMA((1,))],
        plan, down_cat, w_low, w_select, core, far=1)
    sums = call(
        total_kernel,
        [((own, rank), F32), ((rank // replicas, channels), F32), ((doubled // replicas, channels), F32),
         ((states // replicas, channels), F32), ((1, own), F32), ((1, own), F32)], [], got)
    return (grad, *sums[:4], sums[4].reshape(own), sums[5].reshape(own))


def solution(mesh):
    axes = ("ly", "yl", "zh", "x") + REPLICAS
    fine = Mesh(np.asarray(mesh.devices).reshape(2, 2, 4, 4, 4, 2), axes)
    section, dp = axes[:4], REPLICAS
    in_specs = (
        P(None, dp, section),
        P(None, dp, section),
        P(),
        P(section, None),
        P(None, section),
        P(None, section),
        P(None, section),
        P(section),
        P(section),
    )
    out_specs = (
        P(None, dp, section),
        P(section + dp, None),
        P(dp, section),
        P(dp, section),
        P(dp, section),
        P(section + dp),
        P(section + dp),
    )
    return jax.shard_map(per_device, mesh=fine, in_specs=in_specs, out_specs=out_specs, check_vma=False)
```

```python
import functools

import jax
import jax.numpy as jnp
import numpy as np
from jax import lax
from jax.experimental import pallas as pl
from jax.experimental.pallas import tpu as pltpu
from jax.sharding import Mesh
from jax.sharding import PartitionSpec as P

F32, BF16 = jnp.float32, jnp.bfloat16
WIDTH = 640
NN = (((1,), (0,)), ((), ()))
NT = (((1,), (1,)), ((), ()))
TN = (((0,), (0,)), ((), ()))
NEAR = ("yl", "x")
REPLICAS = ("zl", "core")
VMEM_LIMIT = 48 * 1024 * 1024
PROJECT_LIMIT = 60 * 1024 * 1024
SEL_ROWS = 8
TILE = 16


def dot(a, b, dims=NN):
    return lax.dot_general(a, b, dims, preferred_element_type=F32)


def iota(shape, dim):
    return lax.broadcasted_iota(jnp.int32, shape, dim)


def one_hot(mask):
    return jnp.where(mask, 1.0, 0.0).astype(BF16)


def spread_matrix(micro, length):
    shape = (2 * micro * length, micro * length)
    r, c = iota(shape, 0), iota(shape, 1)
    return one_hot((r % micro) * length + r // (2 * micro) == c)


def gather_matrix(micro, length):
    shape = (micro * length, 2 * micro * length)
    r, c = iota(shape, 0), iota(shape, 1)
    return one_hot(r == (c % micro) * length + c // (2 * micro))


def first_half(rows, micro, lanes=128):
    return (iota((rows, lanes), 0) // micro) % 2 == 0


def pick_half(half, wide):
    return jnp.where(half, wide[:, :128], wide[:, 128:])


def two_halves(half, value):
    return jnp.concatenate([jnp.where(half, value, 0.0), jnp.where(half, 0.0, value)], axis=1)


def two_terms(value):
    high = value.astype(BF16)
    return high, (value - high.astype(F32)).astype(BF16)


def fetch(sources, targets, sems):
    copies = [pltpu.make_async_copy(src, dst, sems.at[i]) for i, (src, dst) in enumerate(zip(sources, targets))]
    for copy in copies:
        copy.start()
    return copies


def project_kernel(x_hbm, ws_hbm, wl_hbm, rate_hbm, bias_hbm, skip_hbm, plan_hbm, out_ref, const_ref, order_ref,
                   x_ref, ws_ref, wl_ref, rate_ref, bias_ref, skip_ref, plan_ref, sems):
    copies = fetch((x_hbm, wl_hbm, ws_hbm, rate_hbm, bias_hbm, skip_hbm, plan_hbm),
                   (x_ref, wl_ref, ws_ref, rate_ref, bias_ref, skip_ref, plan_ref), sems)
    rank, doubled, states = wl_ref.shape[1], ws_ref.shape[0], rate_ref.shape[0]
    const_ref[...] = jnp.zeros(const_ref.shape, F32)
    out_ref[:, rank:] = jnp.zeros((x_ref.shape[0], WIDTH - rank), BF16)
    for copy in copies:
        copy.wait()
    x = x_ref[...]
    out_ref[:, :rank] = dot(x, wl_ref[...]).astype(BF16)
    out_ref[:, rank:rank + doubled] = dot(x, ws_ref[...], NT).astype(BF16)
    const_ref[:states, :] = rate_ref[...]
    const_ref[states:states + 1, :] = bias_ref[...]
    const_ref[states + 1:states + 2, :] = skip_ref[...]
    for j in range(plan_ref.shape[0]):
        order_ref[j:j + 1, :] = jnp.full((1, order_ref.shape[1]), plan_ref[j], jnp.int32)


def state_lanes(states):
    shape = (2 * states, 2 * states * 128)
    return one_hot(iota(shape, 1) // 128 == iota(shape, 0))


def grouped_sums(value, count, group=8):
    shape = (group * 128, group)
    ones = one_hot(iota(shape, 0) // 128 == iota(shape, 1))
    parts = [dot(value[:, at * 128:(at + group) * 128], ones) for at in range(0, count, group)]
    return jnp.concatenate(parts, axis=1)


def put_rows(ref, micro, value):
    length = value.shape[0] // micro
    for k in range(2):
        for m in range(micro):
            ref[pl.ds(k * micro + m, length, stride=2 * micro), :] = value[m * length:(m + 1) * length, k * 128:(k + 1) * 128]


def get_rows(ref, micro):
    length = ref.shape[0] // (2 * micro)
    return jnp.concatenate([jnp.concatenate(
        [ref[pl.ds(k * micro + m, length, stride=2 * micro), :] for m in range(micro)], axis=0)
        for k in range(2)], axis=1)


def forward(micro, length, states, rank, x, cat, wd, const_ref, DP, A, H, BC, R, X, D, DX, SG):
    rows = 2 * micro * length
    doubled = 2 * states
    half = first_half(rows, micro)
    lower = first_half(2 * micro, micro)
    T = spread_matrix(micro, length)
    slabs = (length, 2 * micro, 128)
    cat8 = dot(T, cat[:, rank:rank + 2 * doubled]).astype(BF16)
    x8 = pick_half(half, dot(T, x)).reshape(slabs)
    pick = state_lanes(states)
    BC[...] = dot(cat8, jnp.concatenate([pick, pick], axis=0)).reshape(BC.shape)
    put_rows(DP, micro, dot(cat[:, :rank], wd))
    pre8 = DP[...].reshape(slabs)
    pre8 = pre8 + pick_half(lower, const_ref[states:states + 1, :])[None]
    step8 = jax.nn.softplus(pre8)
    X[...] = x8
    D[...] = step8
    DX[...] = step8 * x8
    SG[...] = jax.nn.sigmoid(pre8)
    zero = jnp.zeros((2 * micro, 128), F32)
    for n in range(states):
        R[n] = pick_half(lower, const_ref[n:n + 1, :])
        H[0, n] = zero

    def ahead(t, h):
        d, dx = D[t], DX[t]
        out = []
        for n in range(states):
            a = jnp.exp(-(d * R[n]))
            h_n = a * h[n] + dx * BC[t, :, n * 128:(n + 1) * 128]
            A[t, n] = a
            H[t + 1, n] = h_n
            out.append(h_n)
        return tuple(out)

    lax.fori_loop(0, length, ahead, (zero,) * states, unroll=length)


def backward(micro, length, states, rank, sums, wd, const_ref, G, A, H, BC, R, X, D, DX, SG,
             send_ref, core_ref, products, DP, C):
    rows = 2 * micro * length
    doubled = 2 * states
    half = first_half(rows, micro)
    zero = jnp.zeros((2 * micro, 128), F32)
    skip8 = pick_half(first_half(2 * micro, micro), const_ref[states + 1:states + 2, :])

    def back(i, carry):
        later, bias_acc, skip_acc = carry
        pair = length // 2 - 1 - i
        times = (2 * pair, 2 * pair + 1)
        d, dx, g, xv = ([ref[t] for t in times] for ref in (D, DX, G, X))
        u, w = [zero, zero], [zero, zero]
        passed = []
        for n in range(states):
            rate = R[n]
            b_at, c_at = (slice(at * 128, (at + 1) * 128) for at in (n, states + n))
            h = [H[times[0] + k, n] for k in range(3)]
            lam, q = [None, None], [None, None]
            through = later[n]
            for k in (1, 0):
                lam[k] = BC[times[k], :, c_at] * g[k] + through
                through = A[times[k], n] * lam[k]
                q[k] = through * h[k]
                u[k] = u[k] + lam[k] * BC[times[k], :, b_at]
                w[k] = w[k] + q[k] * rate
            for at, value in ((b_at, [lam[k] * dx[k] for k in range(2)]),
                              (c_at, [g[k] * h[k + 1] for k in range(2)])):
                products[pair, :, at] = jnp.concatenate(value, axis=0).astype(BF16)
            passed.append(through)
            if sums is not None:
                sums[n] = sums[n] + (d[0] * q[0] + d[1] * q[1])
        for k in range(2):
            dpre = (u[k] * xv[k] - w[k]) * SG[times[k]]
            DP[pl.ds(times[k] * 2 * micro, 2 * micro), :] = dpre
            C[pl.ds(times[k] * 2 * micro, 2 * micro), :] = g[k] + (u[k] * d[k] + skip8 * g[k])
            if sums is not None:
                bias_acc, skip_acc = bias_acc + dpre, skip_acc + g[k] * xv[k]
        return tuple(passed), bias_acc, skip_acc

    if sums is not None:
        sums[...] = jnp.zeros(sums.shape, F32)
    start = ((zero,) * states, zero, zero)
    _, bias_acc, skip_acc = lax.fori_loop(0, length // 2, back, start, unroll=length // 2)
    S = gather_matrix(micro, length)
    core_ref[...] = get_rows(C, micro)
    dpre_half = get_rows(DP, micro).astype(BF16)
    send_ref[:, :rank] = dot(dpre_half, wd, NT).astype(BF16)
    high, low = two_terms(grouped_sums(products[...].reshape(rows, doubled * 128), doubled))
    send_ref[:, rank:] = jnp.zeros((micro * length, WIDTH - rank), BF16)
    send_ref[:, rank:rank + doubled] = (dot(S, high) + dot(S, low)).astype(BF16)
    return dpre_half, bias_acc, skip_acc


def tick_kernel(micro, length, states, rank, from_above, *refs):
    x_ref, side_ref, cat_ref, wd_ref, const_ref, *refs = refs
    if from_above:
        above_ref, send_ref, core_ref, dpre_ref, rate_out, ends_ref, *refs = refs
    else:
        send_ref, core_ref, *refs = refs
    G, products, DP, C, *state = refs
    rows = 2 * micro * length
    channels = x_ref.shape[1]
    half = first_half(rows, micro)
    T = spread_matrix(micro, length)
    g8 = pick_half(half, dot(T, side_ref[...]))
    if from_above:
        g8 = g8 + pick_half(half, dot(T, above_ref[...]))
    G[...] = g8.reshape(G.shape)
    forward(micro, length, states, rank, x_ref[...], cat_ref[...], wd_ref[...], const_ref, DP, *state)
    dpre_half, bias_acc, skip_acc = backward(
        micro, length, states, rank, rate_out if from_above else None, wd_ref[...], const_ref, G, *state, send_ref, core_ref, products, DP, C)
    if from_above:
        dpre_ref[...] = dpre_half
        ends_ref[0] = bias_acc
        ends_ref[1] = skip_acc


def layer_grad(cat_ref, wl_ref, ws_ref, core_ref):
    rank, doubled = wl_ref.shape[1], ws_ref.shape[0]
    value = core_ref[...] + dot(cat_ref[:, :rank], wl_ref[...], NT)
    return (value + dot(cat_ref[:, rank:rank + doubled], ws_ref[...])).astype(BF16)


def hand_kernel(cat_ref, wl_ref, ws_ref, core_ref, grad_ref):
    grad_ref[...] = layer_grad(cat_ref, wl_ref, ws_ref, core_ref)


def part_kernel(micro, order_ref, cat_ref, down_ref, x_ref, wl_ref, ws_ref, core_ref, dpre_ref, rate_ref, ends_ref,
                send_ref, grad_ref, small):
    cores, groups, tile, _ = send_ref.shape
    replicas, states = cores * groups, rate_ref.shape[0]
    channels, rank = wl_ref.shape
    own, deep, doubled = channels // replicas, rank // replicas, 2 * states
    share, rate_share = doubled // replicas, states // replicas
    x, down = x_ref[...], down_ref[...]
    low = dot(x, down[:, :rank], TN).astype(BF16)
    delta = dot(cat_ref[:, :rank], dpre_ref[...], TN).astype(BF16)
    select = dot(down[:, rank:rank + doubled], x, TN)
    lower = first_half(2 * micro, micro)

    def row_of(value):
        return jnp.sum(two_halves(lower, value), axis=0, keepdims=True)

    small[...] = jnp.zeros(small.shape, F32)
    for r in range(replicas):
        for k in range(2):
            small[r, k * share:(k + 1) * share, :] = select[r * share:(r + 1) * share, k * 128:(k + 1) * 128]
    for n in range(states):
        row = -row_of(rate_ref[n])
        at = SEL_ROWS + 2 * (n % rate_share)
        small[n // rate_share, at:at + 1, :] = row[:, :128]
        small[n // rate_share, at + 1:at + 2, :] = row[:, 128:]
    at = SEL_ROWS + 2 * rate_share
    for k in range(2):
        row = row_of(ends_ref[k])
        for r in range(replicas):
            small[r, at + k:at + k + 1, :own] = row[:, r * own:(r + 1) * own]
    for r in range(replicas):
        to = (r % cores, r // cores)
        for i in range(own // tile):
            send_ref[*to, :, i * rank:(i + 1) * rank] = low[r * own + i * tile:r * own + (i + 1) * tile]
        first = own // tile * rank
        for i in range(deep // tile):
            lanes = slice(first + i * channels, first + (i + 1) * channels)
            send_ref[*to, :, lanes] = delta[r * deep + i * tile:r * deep + (i + 1) * tile]
        send_ref[*to, :, first + deep // tile * channels:] = small[r].astype(BF16)
    grad = layer_grad(down_ref, wl_ref, ws_ref, core_ref).astype(F32).reshape(grad_ref.shape)
    for j in range(micro):
        which = order_ref[j:j + 1, :]
        value = grad[0]
        for m in range(1, micro):
            value = jnp.where(which == m, grad[m], value)
        grad_ref[j] = value.astype(BF16)


def total_kernel(got_ref, low_ref, delta_ref, sel_ref, rate_ref, bias_ref, skip_ref):
    tile = got_ref.shape[1]
    own, rank = low_ref.shape
    deep, channels = delta_ref.shape

    def summed(start, lanes):
        value = got_ref[0, :, start:start + lanes].astype(F32)
        for r in range(1, got_ref.shape[0]):
            value = value + got_ref[r, :, start:start + lanes].astype(F32)
        return value

    for i in range(own // tile):
        low_ref[i * tile:(i + 1) * tile] = summed(i * rank, rank)
    first = own // tile * rank
    for i in range(deep // tile):
        delta_ref[i * tile:(i + 1) * tile] = summed(first + i * channels, channels)
    small = summed(first + deep // tile * channels, 128)
    rows, share = sel_ref.shape[0], rate_ref.shape[0]
    for k in range(2):
        lanes = slice(k * 128, (k + 1) * 128)
        sel_ref[:, lanes] = small[k * rows:(k + 1) * rows]
        for n in range(share):
            at = SEL_ROWS + 2 * n + k
            rate_ref[n:n + 1, lanes] = small[at:at + 1]
    at = SEL_ROWS + 2 * share
    bias_ref[...] = small[at:at + 1, :own]
    skip_ref[...] = small[at + 1:at + 2, :own]


def call(kernel, outs, scratch, *args, far=0, limit=VMEM_LIMIT):
    vmem = pl.BlockSpec(memory_space=pltpu.VMEM)
    hbm = pl.BlockSpec(memory_space=pl.ANY)
    return pl.pallas_call(
        kernel,
        out_shape=[jax.ShapeDtypeStruct(*out) for out in outs],
        in_specs=[hbm] * far + [vmem] * (len(args) - far),
        out_specs=[vmem] * len(outs),
        scratch_shapes=[pltpu.VMEM(s, F32) if isinstance(s, tuple) else s for s in scratch],
        compiler_params=pltpu.CompilerParams(vmem_limit_bytes=limit),
    )(*args)


def exchange(blocks, axes):
    return lax.all_to_all(blocks, axes, 0, 0)


def to_all(block, axes):
    count = lax.axis_size(axes)
    return exchange(jnp.broadcast_to(block[None], (count,) + block.shape), axes)


def total(blocks):
    return jnp.sum(blocks.astype(F32), axis=0)


def scattered_sum(rows, axes):
    count = lax.axis_size(axes)
    got = exchange(rows.reshape(count, rows.shape[0] // count, rows.shape[1]), axes)
    return total(to_all(total(got).astype(BF16), "zh"))


def per_device(x_saved, side_grad, plan, w_low, w_delta, w_select, decay_rate, delta_bias, skip_gain):
    micro, length, channels = x_saved.shape
    tokens = micro * length
    rank, doubled, states = w_low.shape[1], w_select.shape[0], decay_rate.shape[0]
    replicas = lax.axis_size(REPLICAS)
    x = x_saved.reshape(tokens, channels)
    side = side_grad.reshape(tokens, channels)
    bias, skip = delta_bias.reshape(1, channels), skip_gain.reshape(1, channels)

    sources = (x, w_select, w_low, decay_rate, bias, skip, plan)
    part, const, order = call(
        project_kernel, [((tokens, WIDTH), BF16), ((states + 8, channels), F32), ((8, channels), jnp.int32)],
        [pltpu.VMEM(a.shape, a.dtype) for a in sources[:-1]]
        + [pltpu.SMEM(plan.shape, plan.dtype), pltpu.SemaphoreType.DMA((len(sources),))],
        *sources, far=len(sources), limit=PROJECT_LIMIT)
    summed = scattered_sum(part, NEAR)
    selected = summed[:, rank:rank + doubled]
    high = lax.reduce_precision(selected, 8, 7)
    rest = summed[:, rank + 2 * doubled:]
    packed = jnp.concatenate([summed[:, :rank], high, selected - high, rest], axis=1).astype(BF16)
    cat = to_all(packed, NEAR).reshape(tokens, WIDTH)

    dims = (micro, length, states, rank)
    slab, rows_all = (length, 2 * micro, 128), 2 * tokens
    send_out = ((tokens, WIDTH), BF16)
    scratch = [slab, pltpu.VMEM((length // 2, 4 * micro, doubled * 128), BF16), (rows_all, 128), (rows_all, 128),
               (length, states, 2 * micro, 128), (length + 1, states, 2 * micro, 128),
               (length, 2 * micro, doubled * 128), (states, 2 * micro, 128), slab, slab, slab, slab]
    shared = (x, side, cat, w_delta, const)
    send, core = call(
        functools.partial(tick_kernel, *dims, False), [send_out, ((tokens, channels), F32)], scratch, *shared)
    cat_up = to_all(scattered_sum(send, NEAR).astype(BF16), NEAR).reshape(tokens, WIDTH)
    handed, = call(
        hand_kernel, [((tokens, channels), BF16)], [], cat_up, w_low, w_select, core)
    above = lax.ppermute(handed, "ly", [(1, 0)])

    send, core, dpre, rate_sum, end_sums = call(
        functools.partial(tick_kernel, *dims, True),
        [send_out, ((tokens, channels), F32), ((tokens, channels), BF16), ((states, 2 * micro, 128), F32),
         ((2, 2 * micro, 128), F32)], scratch, *shared, above)
    down_cat = to_all(scattered_sum(send, NEAR).astype(BF16), NEAR).reshape(tokens, WIDTH)

    own, deep = channels // replicas, rank // replicas
    lanes = own // TILE * rank + deep // TILE * channels + 128
    groups, cores = (lax.axis_size(axis) for axis in REPLICAS)
    partials, grad = call(
        functools.partial(part_kernel, micro),
        [((cores, groups, TILE, lanes), BF16), ((micro, length, channels), BF16)], [(replicas, TILE, 128)],
        order, cat, down_cat, x, w_low, w_select, core, dpre, rate_sum, end_sums)
    pairs = total(exchange(partials, "core")).astype(BF16)
    got = exchange(pairs, "zl")
    sums = call(
        total_kernel,
        [((own, rank), F32), ((deep, channels), F32), ((doubled // replicas, channels), F32),
         ((states // replicas, channels), F32), ((1, own), F32), ((1, own), F32)], [], got)
    return (grad, *sums[:4], sums[4].reshape(own), sums[5].reshape(own))


def solution(mesh):
    axes = ("ly", "yl", "zh", "x") + REPLICAS
    fine = Mesh(np.asarray(mesh.devices).reshape(2, 2, 4, 4, 4, 2), axes)
    section, dp = axes[:4], REPLICAS
    in_specs = (
        P(None, dp, section),
        P(None, dp, section),
        P(),
        P(section, None),
        P(None, section),
        P(None, section),
        P(None, section),
        P(section),
        P(section),
    )
    out_specs = (
        P(None, dp, section),
        P(section + dp, None),
        P(dp, section),
        P(dp, section),
        P(dp, section),
        P(section + dp),
        P(section + dp),
    )
    return jax.shard_map(per_device, mesh=fine, in_specs=in_specs, out_specs=out_specs, check_vma=False)
```

```python
import functools

import jax
import jax.numpy as jnp
import numpy as np
from jax import lax
from jax.experimental import pallas as pl
from jax.experimental.pallas import tpu as pltpu
from jax.sharding import Mesh
from jax.sharding import PartitionSpec as P

F32, BF16 = jnp.float32, jnp.bfloat16
WIDTH = 640
NN = (((1,), (0,)), ((), ()))
NT = (((1,), (1,)), ((), ()))
TN = (((0,), (0,)), ((), ()))
NEAR = ("yl", "x")
REPLICAS = ("zl", "core")
VMEM_LIMIT = 24 * 1024 * 1024
PROJECT_LIMIT = 60 * 1024 * 1024
SEL_ROWS = 8
TILE = 16


def dot(a, b, dims=NN):
    return lax.dot_general(a, b, dims, preferred_element_type=F32)


def iota(shape, dim):
    return lax.broadcasted_iota(jnp.int32, shape, dim)


def one_hot(mask):
    return jnp.where(mask, 1.0, 0.0).astype(BF16)


def spread_matrix(micro, length):
    shape = (2 * micro * length, micro * length)
    r, c = iota(shape, 0), iota(shape, 1)
    return one_hot((r % micro) * length + r // (2 * micro) == c)


def gather_matrix(micro, length):
    shape = (micro * length, 2 * micro * length)
    r, c = iota(shape, 0), iota(shape, 1)
    return one_hot(r == (c % micro) * length + c // (2 * micro))


def first_half(rows, micro, lanes=128):
    return (iota((rows, lanes), 0) // micro) % 2 == 0


def pick_half(half, wide):
    return jnp.where(half, wide[:, :128], wide[:, 128:])


def two_halves(half, value):
    return jnp.concatenate([jnp.where(half, value, 0.0), jnp.where(half, 0.0, value)], axis=1)


def two_terms(value):
    high = value.astype(BF16)
    return high, (value - high.astype(F32)).astype(BF16)


def fetch(sources, targets, sems):
    copies = [pltpu.make_async_copy(src, dst, sems.at[i]) for i, (src, dst) in enumerate(zip(sources, targets))]
    for copy in copies:
        copy.start()
    return copies


def project_kernel(x_hbm, ws_hbm, wl_hbm, rate_hbm, bias_hbm, skip_hbm, plan_hbm, out_ref, const_ref,
                   x_ref, ws_ref, wl_ref, rate_ref, bias_ref, skip_ref, plan_ref, sems):
    copies = fetch((x_hbm, wl_hbm, ws_hbm, rate_hbm, bias_hbm, skip_hbm, plan_hbm),
                   (x_ref, wl_ref, ws_ref, rate_ref, bias_ref, skip_ref, plan_ref), sems)
    rank, doubled, states = wl_ref.shape[1], ws_ref.shape[0], rate_ref.shape[0]
    const_ref[...] = jnp.zeros(const_ref.shape, F32)
    out_ref[:, rank:] = jnp.zeros((x_ref.shape[0], WIDTH - rank), BF16)
    for copy in copies:
        copy.wait()
    x = x_ref[...]
    out_ref[:, :rank] = dot(x, wl_ref[...]).astype(BF16)
    out_ref[:, rank:rank + doubled] = dot(x, ws_ref[...], NT).astype(BF16)
    const_ref[:states, :] = rate_ref[...]
    const_ref[states:states + 1, :] = bias_ref[...]
    const_ref[states + 1:states + 2, :] = skip_ref[...]
    for j in range(plan_ref.shape[0]):
        at = states + 2 + j
        const_ref[at:at + 1, :] = jnp.full((1, const_ref.shape[1]), plan_ref[j], jnp.int32).astype(F32)


def state_lanes(states):
    shape = (2 * states, 2 * states * 128)
    return one_hot(iota(shape, 1) // 128 == iota(shape, 0))


def grouped_sums(value, count, group=8):
    shape = (group * 128, group)
    ones = one_hot(iota(shape, 0) // 128 == iota(shape, 1))
    parts = [dot(value[:, at * 128:(at + group) * 128], ones) for at in range(0, count, group)]
    return jnp.concatenate(parts, axis=1)


def put_rows(ref, micro, value):
    length = value.shape[0] // micro
    for k in range(2):
        for m in range(micro):
            ref[pl.ds(k * micro + m, length, stride=2 * micro), :] = value[m * length:(m + 1) * length, k * 128:(k + 1) * 128]


def get_rows(ref, micro):
    length = ref.shape[0] // (2 * micro)
    return jnp.concatenate([jnp.concatenate(
        [ref[pl.ds(k * micro + m, length, stride=2 * micro), :] for m in range(micro)], axis=0)
        for k in range(2)], axis=1)


def prepare(micro, length, states, rank, x, cat, wd, const_ref, DP, Q, R, X, D, DX, SG):
    rows = 2 * micro * length
    doubled = 2 * states
    half = first_half(rows, micro)
    lower = first_half(2 * micro, micro)
    T = spread_matrix(micro, length)
    slabs = (length, 2 * micro, 128)
    cat8 = dot(T, cat[:, rank:rank + 2 * doubled]).astype(BF16)
    x8 = pick_half(half, dot(T, x)).reshape(slabs)
    Q[...] = cat8
    put_rows(DP, micro, dot(cat[:, :rank], wd))
    pre8 = DP[...].reshape(slabs)
    pre8 = pre8 + pick_half(lower, const_ref[states:states + 1, :])[None]
    step8 = jax.nn.softplus(pre8)
    X[...] = x8
    D[...] = step8
    DX[...] = step8 * x8
    SG[...] = jax.nn.sigmoid(pre8)
    for n in range(states):
        R[n] = pick_half(lower, const_ref[n:n + 1, :])
    R[states] = pick_half(lower, const_ref[states + 1:states + 2, :])


def forward(micro, length, states, A, H, BC, Q, R, X, D, DX, SG):
    pick = state_lanes(states)
    BC[...] = dot(Q[...], jnp.concatenate([pick, pick], axis=0)).reshape(BC.shape)
    zero = jnp.zeros((2 * micro, 128), F32)
    for n in range(states):
        H[0, n] = zero

    def ahead(t, h):
        d, dx = D[t], DX[t]
        out = []
        for n in range(states):
            a = jnp.exp(-(d * R[n]))
            h_n = a * h[n] + dx * BC[t, :, n * 128:(n + 1) * 128]
            A[t, n] = a
            H[t + 1, n] = h_n
            out.append(h_n)
        return tuple(out)

    lax.fori_loop(0, length, ahead, (zero,) * states, unroll=length)


def backward(micro, length, states, rank, sums, wd_ref, copies, G, A, H, BC, Q, R, X, D, DX, SG,
             send_ref, core_ref, products, DP, C):
    rows = 2 * micro * length
    doubled = 2 * states
    half = first_half(rows, micro)
    zero = jnp.zeros((2 * micro, 128), F32)
    skip8 = R[states]

    def back(i, carry):
        later, bias_acc, skip_acc = carry
        pair = length // 2 - 1 - i
        times = (2 * pair, 2 * pair + 1)
        d, dx, g, xv = ([ref[t] for t in times] for ref in (D, DX, G, X))
        u, w = [zero, zero], [zero, zero]
        passed = []
        for n in range(states):
            rate = R[n]
            b_at, c_at = (slice(at * 128, (at + 1) * 128) for at in (n, states + n))
            h = [H[times[0] + k, n] for k in range(3)]
            lam, q = [None, None], [None, None]
            through = later[n]
            for k in (1, 0):
                lam[k] = BC[times[k], :, c_at] * g[k] + through
                through = A[times[k], n] * lam[k]
                q[k] = through * h[k]
                u[k] = u[k] + lam[k] * BC[times[k], :, b_at]
                w[k] = w[k] + q[k] * rate
            for at, value in ((b_at, [lam[k] * dx[k] for k in range(2)]),
                              (c_at, [g[k] * h[k + 1] for k in range(2)])):
                products[pair, :, at] = jnp.concatenate(value, axis=0).astype(BF16)
            passed.append(through)
            if sums is not None:
                sums[n] = sums[n] + (d[0] * q[0] + d[1] * q[1])
        for k in range(2):
            dpre = (u[k] * xv[k] - w[k]) * SG[times[k]]
            DP[pl.ds(times[k] * 2 * micro, 2 * micro), :] = dpre
            C[pl.ds(times[k] * 2 * micro, 2 * micro), :] = g[k] + (u[k] * d[k] + skip8 * g[k])
            if sums is not None:
                bias_acc, skip_acc = bias_acc + dpre, skip_acc + g[k] * xv[k]
        return tuple(passed), bias_acc, skip_acc

    if sums is not None:
        sums[...] = jnp.zeros(sums.shape, F32)
    start = ((zero,) * states, zero, zero)
    _, bias_acc, skip_acc = lax.fori_loop(0, length // 2, back, start, unroll=length // 2)
    S = gather_matrix(micro, length)
    core_ref[...] = get_rows(C, micro)
    dpre_half = get_rows(DP, micro).astype(BF16)
    for copy in copies:
        copy.wait()
    send_ref[:, :rank] = dot(dpre_half, wd_ref[...], NT).astype(BF16)
    high, low = two_terms(grouped_sums(products[...].reshape(rows, doubled * 128), doubled))
    send_ref[:, rank:] = jnp.zeros((micro * length, WIDTH - rank), BF16)
    send_ref[:, rank:rank + doubled] = (dot(S, high) + dot(S, low)).astype(BF16)
    return dpre_half, bias_acc, skip_acc


def spread_rows(micro, length, ref):
    half = first_half(2 * micro * length, micro)
    return pick_half(half, dot(spread_matrix(micro, length), ref[...])).reshape(length, 2 * micro, 128)


def upper_kernel(micro, length, states, rank, x_ref, side_ref, cat_ref, wd_ref, const_ref, send_ref, core_ref,
                 G, products, DP, C, *state):
    G[...] = spread_rows(micro, length, side_ref)
    prepare(micro, length, states, rank, x_ref[...], cat_ref[...], wd_ref[...], const_ref, DP, *state[3:])
    forward(micro, length, states, *state)
    backward(micro, length, states, rank, None, wd_ref, (), G, *state, send_ref, core_ref, products, DP, C)


def ahead_kernel(micro, length, states, rank, x_any, side_any, cat_any, wd_any, const_any, *refs):
    *outs, DP, x_ref, side_ref, cat_ref, wd_ref, const_ref, sems = refs
    for copy in fetch((x_any, side_any, cat_any, wd_any, const_any), (x_ref, side_ref, cat_ref, wd_ref, const_ref), sems):
        copy.wait()
    outs[0][...] = spread_rows(micro, length, side_ref)
    prepare(micro, length, states, rank, x_ref[...], cat_ref[...], wd_ref[...], const_ref, DP, *outs[1:])


def lower_kernel(micro, length, states, rank, wd_any, above_ref, side_ref, *refs):
    *ready, send_ref, core_ref, dpre_ref, rate_ref, ends_ref, G, products, DP, C, A, H, BC, wd_ref, sems = refs
    state = (A, H, BC, *ready)
    copies = fetch((wd_any,), (wd_ref,), sems)
    G[...] = side_ref[...] + spread_rows(micro, length, above_ref)
    forward(micro, length, states, *state)
    dpre_half, bias_acc, skip_acc = backward(
        micro, length, states, rank, rate_ref, wd_ref, copies, G, *state, send_ref, core_ref, products, DP, C)
    dpre_ref[...] = dpre_half
    ends_ref[0] = bias_acc
    ends_ref[1] = skip_acc


def layer_grad(cat_ref, wl_ref, ws_ref, core_ref):
    rank, doubled = wl_ref.shape[1], ws_ref.shape[0]
    value = core_ref[...] + dot(cat_ref[:, :rank], wl_ref[...], NT)
    return (value + dot(cat_ref[:, rank:rank + doubled], ws_ref[...])).astype(BF16)


def hand_kernel(cat_ref, wl_ref, ws_ref, core_ref, grad_ref):
    grad_ref[...] = layer_grad(cat_ref, wl_ref, ws_ref, core_ref)


def part_kernel(micro, const_ref, cat_ref, down_ref, x_ref, wl_ref, ws_ref, core_ref, dpre_ref, rate_ref, ends_ref,
                send_ref, grad_ref, small):
    cores, groups, tile, _ = send_ref.shape
    replicas, states = cores * groups, rate_ref.shape[0]
    channels, rank = wl_ref.shape
    own, deep, doubled = channels // replicas, rank // replicas, 2 * states
    share, rate_share = doubled // replicas, states // replicas
    x, down = x_ref[...], down_ref[...]
    low = dot(x, down[:, :rank], TN).astype(BF16)
    delta = dot(cat_ref[:, :rank], dpre_ref[...], TN).astype(BF16)
    select = dot(down[:, rank:rank + doubled], x, TN)
    lower = first_half(2 * micro, micro)

    def row_of(value):
        return jnp.sum(two_halves(lower, value), axis=0, keepdims=True)

    small[...] = jnp.zeros(small.shape, F32)
    for r in range(replicas):
        for k in range(2):
            small[r, k * share:(k + 1) * share, :] = select[r * share:(r + 1) * share, k * 128:(k + 1) * 128]
    for n in range(states):
        row = -row_of(rate_ref[n])
        at = SEL_ROWS + 2 * (n % rate_share)
        small[n // rate_share, at:at + 1, :] = row[:, :128]
        small[n // rate_share, at + 1:at + 2, :] = row[:, 128:]
    at = SEL_ROWS + 2 * rate_share
    for k in range(2):
        row = row_of(ends_ref[k])
        for r in range(replicas):
            small[r, at + k:at + k + 1, :own] = row[:, r * own:(r + 1) * own]
    for r in range(replicas):
        to = (r % cores, r // cores)
        for i in range(own // tile):
            send_ref[*to, :, i * rank:(i + 1) * rank] = low[r * own + i * tile:r * own + (i + 1) * tile]
        first = own // tile * rank
        for i in range(deep // tile):
            lanes = slice(first + i * channels, first + (i + 1) * channels)
            send_ref[*to, :, lanes] = delta[r * deep + i * tile:r * deep + (i + 1) * tile]
        send_ref[*to, :, first + deep // tile * channels:] = small[r].astype(BF16)
    grad = layer_grad(down_ref, wl_ref, ws_ref, core_ref).astype(F32).reshape(grad_ref.shape)
    for j in range(micro):
        which = const_ref[states + 2 + j:states + 3 + j, :]
        value = grad[0]
        for m in range(1, micro):
            value = jnp.where(which == float(m), grad[m], value)
        grad_ref[j] = value.astype(BF16)


def total_kernel(got_ref, low_ref, delta_ref, sel_ref, rate_ref, bias_ref, skip_ref):
    tile = got_ref.shape[1]
    own, rank = low_ref.shape
    deep, channels = delta_ref.shape

    def summed(start, lanes):
        value = got_ref[0, :, start:start + lanes].astype(F32)
        for r in range(1, got_ref.shape[0]):
            value = value + got_ref[r, :, start:start + lanes].astype(F32)
        return value

    for i in range(own // tile):
        low_ref[i * tile:(i + 1) * tile] = summed(i * rank, rank)
    first = own // tile * rank
    for i in range(deep // tile):
        delta_ref[i * tile:(i + 1) * tile] = summed(first + i * channels, channels)
    small = summed(first + deep // tile * channels, 128)
    rows, share = sel_ref.shape[0], rate_ref.shape[0]
    for k in range(2):
        lanes = slice(k * 128, (k + 1) * 128)
        sel_ref[:, lanes] = small[k * rows:(k + 1) * rows]
        for n in range(share):
            at = SEL_ROWS + 2 * n + k
            rate_ref[n:n + 1, lanes] = small[at:at + 1]
    at = SEL_ROWS + 2 * share
    bias_ref[...] = small[at:at + 1, :own]
    skip_ref[...] = small[at + 1:at + 2, :own]


def call(kernel, outs, scratch, *args, far=0, limit=VMEM_LIMIT):
    vmem = pl.BlockSpec(memory_space=pltpu.VMEM)
    hbm = pl.BlockSpec(memory_space=pl.ANY)
    return pl.pallas_call(
        kernel,
        out_shape=[jax.ShapeDtypeStruct(*out) for out in outs],
        in_specs=[hbm] * far + [vmem] * (len(args) - far),
        out_specs=[vmem] * len(outs),
        scratch_shapes=[pltpu.VMEM(s, F32) if isinstance(s, tuple) else s for s in scratch],
        compiler_params=pltpu.CompilerParams(vmem_limit_bytes=limit),
    )(*args)


def exchange(blocks, axes):
    return lax.all_to_all(blocks, axes, 0, 0)


def to_all(block, axes):
    count = lax.axis_size(axes)
    return exchange(jnp.broadcast_to(block[None], (count,) + block.shape), axes)


def total(blocks):
    return jnp.sum(blocks.astype(F32), axis=0)


def scattered_sum(rows, axes):
    count = lax.axis_size(axes)
    got = exchange(rows.reshape(count, rows.shape[0] // count, rows.shape[1]), axes)
    return total(to_all(total(got).astype(BF16), "zh"))


def per_device(x_saved, side_grad, plan, w_low, w_delta, w_select, decay_rate, delta_bias, skip_gain):
    micro, length, channels = x_saved.shape
    tokens = micro * length
    rank, doubled, states = w_low.shape[1], w_select.shape[0], decay_rate.shape[0]
    replicas = lax.axis_size(REPLICAS)
    x = x_saved.reshape(tokens, channels)
    side = side_grad.reshape(tokens, channels)
    bias, skip = delta_bias.reshape(1, channels), skip_gain.reshape(1, channels)

    sources = (x, w_select, w_low, decay_rate, bias, skip, plan)
    part, const = call(
        project_kernel, [((tokens, WIDTH), BF16), ((states + 8, channels), F32)],
        [pltpu.VMEM(a.shape, a.dtype) for a in sources[:-1]]
        + [pltpu.SMEM(plan.shape, plan.dtype), pltpu.SemaphoreType.DMA((len(sources),))],
        *sources, far=len(sources), limit=PROJECT_LIMIT)
    summed = scattered_sum(part, NEAR)
    selected = summed[:, rank:rank + doubled]
    high = lax.reduce_precision(selected, 8, 7)
    rest = summed[:, rank + 2 * doubled:]
    packed = jnp.concatenate([summed[:, :rank], high, selected - high, rest], axis=1).astype(BF16)
    cat = to_all(packed, NEAR).reshape(tokens, WIDTH)

    dims = (micro, length, states, rank)
    slab, rows_all = (length, 2 * micro, 128), (2 * tokens, 128)
    send_out, grad_out = ((tokens, WIDTH), BF16), (tokens, channels)
    scratch = [slab, pltpu.VMEM((length // 2, 4 * micro, doubled * 128), BF16), rows_all, rows_all]
    state = [(length, states, 2 * micro, 128), (length + 1, states, 2 * micro, 128),
             (length, 2 * micro, doubled * 128), (states + 1, 2 * micro, 128), slab, slab, slab, slab]
    state.insert(3, pltpu.VMEM((2 * tokens, 2 * doubled), BF16))
    send, core = call(
        functools.partial(upper_kernel, *dims), [send_out, (grad_out, F32)], scratch + state,
        x, side, cat, w_delta, const)
    cat_up = to_all(scattered_sum(send, NEAR).astype(BF16), NEAR).reshape(tokens, WIDTH)
    handed, = call(hand_kernel, [(grad_out, BF16)], [], cat_up, w_low, w_select, core)
    above = lax.ppermute(handed, "ly", [(1, 0)])
    held_cat, _ = lax.optimization_barrier((cat, handed))
    early = (x, side, held_cat, w_delta, const)
    ahead = call(
        functools.partial(ahead_kernel, *dims), [(slab, F32), ((2 * tokens, 2 * doubled), BF16)] + [(shape, F32) for shape in state[4:]],
        [rows_all] + [pltpu.VMEM(a.shape, a.dtype) for a in early] + [pltpu.SemaphoreType.DMA((len(early),))],
        *early, far=len(early))

    send, core, dpre, rate_sum, end_sums = call(
        functools.partial(lower_kernel, *dims),
        [send_out, (grad_out, F32), (grad_out, BF16), ((states, 2 * micro, 128), F32), ((2, 2 * micro, 128), F32)],
        scratch + state[:3] + [pltpu.VMEM(w_delta.shape, BF16), pltpu.SemaphoreType.DMA((1,))], w_delta, above, *ahead, far=1)
    down_cat = to_all(scattered_sum(send, NEAR).astype(BF16), NEAR).reshape(tokens, WIDTH)

    own, deep = channels // replicas, rank // replicas
    lanes = own // TILE * rank + deep // TILE * channels + 128
    groups, cores = (lax.axis_size(axis) for axis in REPLICAS)
    partials, grad = call(
        functools.partial(part_kernel, micro),
        [((cores, groups, TILE, lanes), BF16), ((micro, length, channels), BF16)], [(replicas, TILE, 128)],
        const, cat, down_cat, x, w_low, w_select, core, dpre, rate_sum, end_sums)
    pairs = total(exchange(partials, "core")).astype(BF16)
    got = exchange(pairs, "zl")
    sums = call(
        total_kernel,
        [((own, rank), F32), ((deep, channels), F32), ((doubled // replicas, channels), F32),
         ((states // replicas, channels), F32), ((1, own), F32), ((1, own), F32)], [], got)
    return (grad, *sums[:4], sums[4].reshape(own), sums[5].reshape(own))


def solution(mesh):
    axes = ("ly", "yl", "zh", "x") + REPLICAS
    fine = Mesh(np.asarray(mesh.devices).reshape(2, 2, 4, 4, 4, 2), axes)
    section, dp = axes[:4], REPLICAS
    in_specs = (
        P(None, dp, section),
        P(None, dp, section),
        P(),
        P(section, None),
        P(None, section),
        P(None, section),
        P(None, section),
        P(section),
        P(section),
    )
    out_specs = (
        P(None, dp, section),
        P(section + dp, None),
        P(dp, section),
        P(dp, section),
        P(dp, section),
        P(section + dp),
        P(section + dp),
    )
    return jax.shard_map(per_device, mesh=fine, in_specs=in_specs, out_specs=out_specs, check_vma=False)
```

```python
import functools

import jax
import jax.numpy as jnp
import numpy as np
from jax import lax
from jax.experimental import pallas as pl
from jax.experimental.pallas import tpu as pltpu
from jax.sharding import Mesh
from jax.sharding import PartitionSpec as P

F32, BF16 = jnp.float32, jnp.bfloat16
WIDTH = 640
NN = (((1,), (0,)), ((), ()))
NT = (((1,), (1,)), ((), ()))
TN = (((0,), (0,)), ((), ()))
NEAR = ("yl", "x")
REPLICAS = ("zl", "core")
VMEM_LIMIT = 24 * 1024 * 1024
PROJECT_LIMIT = 60 * 1024 * 1024
SEL_ROWS = 8
TILE = 16


def dot(a, b, dims=NN):
    return lax.dot_general(a, b, dims, preferred_element_type=F32)


def iota(shape, dim):
    return lax.broadcasted_iota(jnp.int32, shape, dim)


def one_hot(mask):
    return jnp.where(mask, 1.0, 0.0).astype(BF16)


def spread_matrix(micro, length):
    shape = (2 * micro * length, micro * length)
    r, c = iota(shape, 0), iota(shape, 1)
    return one_hot((r % micro) * length + r // (2 * micro) == c)


def gather_matrix(micro, length):
    shape = (micro * length, 2 * micro * length)
    r, c = iota(shape, 0), iota(shape, 1)
    return one_hot(r == (c % micro) * length + c // (2 * micro))


def first_half(rows, micro, lanes=128):
    return (iota((rows, lanes), 0) // micro) % 2 == 0


def pick_half(half, wide):
    return jnp.where(half, wide[:, :128], wide[:, 128:])


def two_halves(half, value):
    return jnp.concatenate([jnp.where(half, value, 0.0), jnp.where(half, 0.0, value)], axis=1)


def two_terms(value):
    high = value.astype(BF16)
    return high, (value - high.astype(F32)).astype(BF16)


def fetch(sources, targets, sems):
    copies = [pltpu.make_async_copy(src, dst, sems.at[i]) for i, (src, dst) in enumerate(zip(sources, targets))]
    for copy in copies:
        copy.start()
    return copies


def project_kernel(x_hbm, ws_hbm, wl_hbm, rate_hbm, bias_hbm, skip_hbm, plan_hbm, out_ref, const_ref,
                   x_ref, ws_ref, wl_ref, rate_ref, bias_ref, skip_ref, plan_ref, sems):
    copies = fetch((x_hbm, wl_hbm, ws_hbm, rate_hbm, bias_hbm, skip_hbm, plan_hbm),
                   (x_ref, wl_ref, ws_ref, rate_ref, bias_ref, skip_ref, plan_ref), sems)
    rank, doubled, states = wl_ref.shape[1], ws_ref.shape[0], rate_ref.shape[0]
    const_ref[...] = jnp.zeros(const_ref.shape, F32)
    out_ref[:, rank:] = jnp.zeros((x_ref.shape[0], WIDTH - rank), BF16)
    for copy in copies:
        copy.wait()
    x = x_ref[...]
    out_ref[:, :rank] = dot(x, wl_ref[...]).astype(BF16)
    out_ref[:, rank:rank + doubled] = dot(x, ws_ref[...], NT).astype(BF16)
    const_ref[:states, :] = rate_ref[...]
    const_ref[states:states + 1, :] = bias_ref[...]
    const_ref[states + 1:states + 2, :] = skip_ref[...]
    for j in range(plan_ref.shape[0]):
        at = states + 2 + j
        const_ref[at:at + 1, :] = jnp.full((1, const_ref.shape[1]), plan_ref[j], jnp.int32).astype(F32)


def state_lanes(states):
    shape = (2 * states, 2 * states * 128)
    return one_hot(iota(shape, 1) // 128 == iota(shape, 0))


def grouped_sums(value, count, group=8):
    shape = (group * 128, group)
    ones = one_hot(iota(shape, 0) // 128 == iota(shape, 1))
    parts = [dot(value[:, at * 128:(at + group) * 128], ones) for at in range(0, count, group)]
    return jnp.concatenate(parts, axis=1)


def put_rows(ref, micro, value):
    length = value.shape[0] // micro
    for k in range(2):
        for m in range(micro):
            ref[pl.ds(k * micro + m, length, stride=2 * micro), :] = value[m * length:(m + 1) * length, k * 128:(k + 1) * 128]


def get_rows(ref, micro):
    length = ref.shape[0] // (2 * micro)
    return jnp.concatenate([jnp.concatenate(
        [ref[pl.ds(k * micro + m, length, stride=2 * micro), :] for m in range(micro)], axis=0)
        for k in range(2)], axis=1)


def prepare(micro, length, states, rank, x, cat, wd, const_ref, DP, Q, R, X, D, DX, SG):
    rows = 2 * micro * length
    doubled = 2 * states
    half = first_half(rows, micro)
    lower = first_half(2 * micro, micro)
    T = spread_matrix(micro, length)
    slabs = (length, 2 * micro, 128)
    cat8 = dot(T, cat[:, rank:rank + 2 * doubled]).astype(BF16)
    x8 = pick_half(half, dot(T, x)).reshape(slabs)
    Q[...] = cat8
    put_rows(DP, micro, dot(cat[:, :rank], wd))
    pre8 = DP[...].reshape(slabs)
    pre8 = pre8 + pick_half(lower, const_ref[states:states + 1, :])[None]
    step8 = jax.nn.softplus(pre8)
    X[...] = x8
    D[...] = step8
    DX[...] = step8 * x8
    SG[...] = jax.nn.sigmoid(pre8)
    for n in range(states):
        R[n] = pick_half(lower, const_ref[n:n + 1, :])
    R[states] = pick_half(lower, const_ref[states + 1:states + 2, :])


def forward(micro, length, states, A, H, BC, Q, R, X, D, DX, SG):
    pick = state_lanes(states)
    BC[...] = dot(Q[...], jnp.concatenate([pick, pick], axis=0)).reshape(BC.shape)
    zero = jnp.zeros((2 * micro, 128), F32)
    for n in range(states):
        H[0, n] = zero

    def ahead(t, h):
        d, dx = D[t], DX[t]
        out = []
        for n in range(states):
            a = jnp.exp(-(d * R[n]))
            h_n = a * h[n] + dx * BC[t, :, n * 128:(n + 1) * 128]
            A[t, n] = a
            H[t + 1, n] = h_n
            out.append(h_n)
        return tuple(out)

    lax.fori_loop(0, length, ahead, (zero,) * states, unroll=length)


def backward(micro, length, states, rank, sums, wd_ref, copies, G, A, H, BC, Q, R, X, D, DX, SG,
             send_ref, core_ref, products, DP, C):
    rows = 2 * micro * length
    doubled = 2 * states
    half = first_half(rows, micro)
    zero = jnp.zeros((2 * micro, 128), F32)
    skip8 = R[states]

    def back(i, carry):
        later, bias_acc, skip_acc = carry
        pair = length // 2 - 1 - i
        times = (2 * pair, 2 * pair + 1)
        d, dx, g, xv = ([ref[t] for t in times] for ref in (D, DX, G, X))
        u, w = [zero, zero], [zero, zero]
        passed = []
        for n in range(states):
            rate = R[n]
            b_at, c_at = (slice(at * 128, (at + 1) * 128) for at in (n, states + n))
            h = [H[times[0] + k, n] for k in range(3)]
            lam, q = [None, None], [None, None]
            through = later[n]
            for k in (1, 0):
                lam[k] = BC[times[k], :, c_at] * g[k] + through
                through = A[times[k], n] * lam[k]
                q[k] = through * h[k]
                u[k] = u[k] + lam[k] * BC[times[k], :, b_at]
                w[k] = w[k] + q[k] * rate
            for at, value in ((b_at, [lam[k] * dx[k] for k in range(2)]),
                              (c_at, [g[k] * h[k + 1] for k in range(2)])):
                products[pair, :, at] = jnp.concatenate(value, axis=0).astype(BF16)
            passed.append(through)
            if sums is not None:
                sums[n] = sums[n] + (d[0] * q[0] + d[1] * q[1])
        for k in range(2):
            dpre = (u[k] * xv[k] - w[k]) * SG[times[k]]
            DP[pl.ds(times[k] * 2 * micro, 2 * micro), :] = dpre
            C[pl.ds(times[k] * 2 * micro, 2 * micro), :] = g[k] + (u[k] * d[k] + skip8 * g[k])
            if sums is not None:
                bias_acc, skip_acc = bias_acc + dpre, skip_acc + g[k] * xv[k]
        return tuple(passed), bias_acc, skip_acc

    if sums is not None:
        sums[...] = jnp.zeros(sums.shape, F32)
    start = ((zero,) * states, zero, zero)
    _, bias_acc, skip_acc = lax.fori_loop(0, length // 2, back, start, unroll=length // 2)
    S = gather_matrix(micro, length)
    core_ref[...] = get_rows(C, micro)
    dpre_half = get_rows(DP, micro).astype(BF16)
    for copy in copies:
        copy.wait()
    send_ref[:, :rank] = dot(dpre_half, wd_ref[...], NT).astype(BF16)
    high, low = two_terms(grouped_sums(products[...].reshape(rows, doubled * 128), doubled))
    send_ref[:, rank:] = jnp.zeros((micro * length, WIDTH - rank), BF16)
    send_ref[:, rank:rank + doubled] = (dot(S, high) + dot(S, low)).astype(BF16)
    return dpre_half, bias_acc, skip_acc


def spread_rows(micro, length, ref):
    half = first_half(2 * micro * length, micro)
    return pick_half(half, dot(spread_matrix(micro, length), ref[...])).reshape(length, 2 * micro, 128)


def upper_kernel(micro, length, states, rank, x_ref, side_ref, cat_ref, wd_ref, const_ref, send_ref, core_ref,
                 G, products, DP, C, *state):
    G[...] = spread_rows(micro, length, side_ref)
    prepare(micro, length, states, rank, x_ref[...], cat_ref[...], wd_ref[...], const_ref, DP, *state[3:])
    forward(micro, length, states, *state)
    backward(micro, length, states, rank, None, wd_ref, (), G, *state, send_ref, core_ref, products, DP, C)


def ahead_kernel(micro, length, states, rank, x_any, side_any, cat_any, wd_any, const_any, *refs):
    *outs, DP, x_ref, side_ref, cat_ref, wd_ref, const_ref, sems = refs
    for copy in fetch((x_any, side_any, cat_any, wd_any, const_any), (x_ref, side_ref, cat_ref, wd_ref, const_ref), sems):
        copy.wait()
    outs[0][...] = spread_rows(micro, length, side_ref)
    prepare(micro, length, states, rank, x_ref[...], cat_ref[...], wd_ref[...], const_ref, DP, *outs[1:])


def lower_kernel(micro, length, states, rank, wd_any, above_ref, side_ref, *refs):
    *ready, send_ref, core_ref, dpre_ref, rate_ref, ends_ref, G, products, DP, C, A, H, BC, wd_ref, sems = refs
    state = (A, H, BC, *ready)
    copies = fetch((wd_any,), (wd_ref,), sems)
    G[...] = side_ref[...] + spread_rows(micro, length, above_ref)
    forward(micro, length, states, *state)
    dpre_half, bias_acc, skip_acc = backward(
        micro, length, states, rank, rate_ref, wd_ref, copies, G, *state, send_ref, core_ref, products, DP, C)
    dpre_ref[...] = dpre_half
    ends_ref[0] = bias_acc
    ends_ref[1] = skip_acc


def layer_grad(cat_ref, wl_ref, ws_ref, core_ref):
    rank, doubled = wl_ref.shape[1], ws_ref.shape[0]
    value = core_ref[...] + dot(cat_ref[:, :rank], wl_ref[...], NT)
    return (value + dot(cat_ref[:, rank:rank + doubled], ws_ref[...])).astype(BF16)


def hand_kernel(cat_ref, wl_ref, ws_ref, core_ref, grad_ref):
    grad_ref[...] = layer_grad(cat_ref, wl_ref, ws_ref, core_ref)


def part_kernel(micro, cat_ref, down_ref, x_ref, dpre_ref, rate_ref, ends_ref, keep_ref, give_ref, small):
    groups, tile, _ = keep_ref.shape
    cores = small.shape[0] // groups
    replicas, states = cores * groups, rate_ref.shape[0]
    channels, rank = x_ref.shape[1], cat_ref.shape[1] // 128 * 128 - 128
    own, deep, doubled = channels // replicas, rank // replicas, 2 * states
    share, rate_share = doubled // replicas, states // replicas
    x, down = x_ref[...], down_ref[...]
    low = dot(x, down[:, :rank], TN).astype(BF16)
    delta = dot(cat_ref[:, :rank], dpre_ref[...], TN).astype(BF16)
    select = dot(down[:, rank:rank + doubled], x, TN)
    lower = first_half(2 * micro, micro)

    def row_of(value):
        return jnp.sum(two_halves(lower, value), axis=0, keepdims=True)

    small[...] = jnp.zeros(small.shape, F32)
    for r in range(replicas):
        for k in range(2):
            small[r, k * share:(k + 1) * share, :] = select[r * share:(r + 1) * share, k * 128:(k + 1) * 128]
    for n in range(states):
        row = -row_of(rate_ref[n])
        at = SEL_ROWS + 2 * (n % rate_share)
        small[n // rate_share, at:at + 1, :] = row[:, :128]
        small[n // rate_share, at + 1:at + 2, :] = row[:, 128:]
    at = SEL_ROWS + 2 * rate_share
    for k in range(2):
        row = row_of(ends_ref[k])
        for r in range(replicas):
            small[r, at + k:at + k + 1, :own] = row[:, r * own:(r + 1) * own]
    first = own // tile * rank

    def fill(ref, core):
        for z in range(groups):
            r = z * cores + core
            for i in range(own // tile):
                ref[z, :, i * rank:(i + 1) * rank] = low[r * own + i * tile:r * own + (i + 1) * tile]
            for i in range(deep // tile):
                lanes = slice(first + i * channels, first + (i + 1) * channels)
                ref[z, :, lanes] = delta[r * deep + i * tile:r * deep + (i + 1) * tile]
            ref[z, :, first + deep // tile * channels:] = small[r].astype(BF16)

    mine = lax.axis_index("core")
    for core in range(cores):
        @pl.when(mine == core)
        def _():
            fill(keep_ref, core)
            fill(give_ref, 1 - core)


def order_kernel(states, const_ref, down_ref, wl_ref, ws_ref, core_ref, grad_ref):
    micro = grad_ref.shape[0]
    grad = layer_grad(down_ref, wl_ref, ws_ref, core_ref).astype(F32).reshape(grad_ref.shape)
    for j in range(micro):
        which = const_ref[states + 2 + j:states + 3 + j, :]
        value = grad[0]
        for m in range(1, micro):
            value = jnp.where(which == float(m), grad[m], value)
        grad_ref[j] = value.astype(BF16)


def total_kernel(got_ref, low_ref, delta_ref, sel_ref, rate_ref, bias_ref, skip_ref):
    tile = got_ref.shape[1]
    own, rank = low_ref.shape
    deep, channels = delta_ref.shape

    def summed(start, lanes):
        value = got_ref[0, :, start:start + lanes].astype(F32)
        for r in range(1, got_ref.shape[0]):
            value = value + got_ref[r, :, start:start + lanes].astype(F32)
        return value

    for i in range(own // tile):
        low_ref[i * tile:(i + 1) * tile] = summed(i * rank, rank)
    first = own // tile * rank
    for i in range(deep // tile):
        delta_ref[i * tile:(i + 1) * tile] = summed(first + i * channels, channels)
    small = summed(first + deep // tile * channels, 128)
    rows, share = sel_ref.shape[0], rate_ref.shape[0]
    for k in range(2):
        lanes = slice(k * 128, (k + 1) * 128)
        sel_ref[:, lanes] = small[k * rows:(k + 1) * rows]
        for n in range(share):
            at = SEL_ROWS + 2 * n + k
            rate_ref[n:n + 1, lanes] = small[at:at + 1]
    at = SEL_ROWS + 2 * share
    bias_ref[...] = small[at:at + 1, :own]
    skip_ref[...] = small[at + 1:at + 2, :own]


def call(kernel, outs, scratch, *args, far=0, limit=VMEM_LIMIT):
    vmem = pl.BlockSpec(memory_space=pltpu.VMEM)
    hbm = pl.BlockSpec(memory_space=pl.ANY)
    return pl.pallas_call(
        kernel,
        out_shape=[jax.ShapeDtypeStruct(*out) for out in outs],
        in_specs=[hbm] * far + [vmem] * (len(args) - far),
        out_specs=[vmem] * len(outs),
        scratch_shapes=[pltpu.VMEM(s, F32) if isinstance(s, tuple) else s for s in scratch],
        compiler_params=pltpu.CompilerParams(vmem_limit_bytes=limit),
    )(*args)


def exchange(blocks, axes):
    return lax.all_to_all(blocks, axes, 0, 0)


def to_all(block, axes):
    count = lax.axis_size(axes)
    return exchange(jnp.broadcast_to(block[None], (count,) + block.shape), axes)


def total(blocks):
    return jnp.sum(blocks.astype(F32), axis=0)


def scattered_sum(rows, axes):
    count = lax.axis_size(axes)
    got = exchange(rows.reshape(count, rows.shape[0] // count, rows.shape[1]), axes)
    return total(to_all(total(got).astype(BF16), "zh"))


def per_device(x_saved, side_grad, plan, w_low, w_delta, w_select, decay_rate, delta_bias, skip_gain):
    micro, length, channels = x_saved.shape
    tokens = micro * length
    rank, doubled, states = w_low.shape[1], w_select.shape[0], decay_rate.shape[0]
    replicas = lax.axis_size(REPLICAS)
    x = x_saved.reshape(tokens, channels)
    side = side_grad.reshape(tokens, channels)
    bias, skip = delta_bias.reshape(1, channels), skip_gain.reshape(1, channels)

    sources = (x, w_select, w_low, decay_rate, bias, skip, plan)
    part, const = call(
        project_kernel, [((tokens, WIDTH), BF16), ((states + 8, channels), F32)],
        [pltpu.VMEM(a.shape, a.dtype) for a in sources[:-1]]
        + [pltpu.SMEM(plan.shape, plan.dtype), pltpu.SemaphoreType.DMA((len(sources),))],
        *sources, far=len(sources), limit=PROJECT_LIMIT)
    summed = scattered_sum(part, NEAR)
    selected = summed[:, rank:rank + doubled]
    high = lax.reduce_precision(selected, 8, 7)
    rest = summed[:, rank + 2 * doubled:]
    packed = jnp.concatenate([summed[:, :rank], high, selected - high, rest], axis=1).astype(BF16)
    cat = to_all(packed, NEAR).reshape(tokens, WIDTH)

    dims = (micro, length, states, rank)
    slab, rows_all = (length, 2 * micro, 128), (2 * tokens, 128)
    send_out, grad_out = ((tokens, WIDTH), BF16), (tokens, channels)
    scratch = [slab, pltpu.VMEM((length // 2, 4 * micro, doubled * 128), BF16), rows_all, rows_all]
    state = [(length, states, 2 * micro, 128), (length + 1, states, 2 * micro, 128),
             (length, 2 * micro, doubled * 128), (states + 1, 2 * micro, 128), slab, slab, slab, slab]
    state.insert(3, pltpu.VMEM((2 * tokens, 2 * doubled), BF16))
    send, core = call(
        functools.partial(upper_kernel, *dims), [send_out, (grad_out, F32)], scratch + state,
        x, side, cat, w_delta, const)
    cat_up = to_all(scattered_sum(send, NEAR).astype(BF16), NEAR).reshape(tokens, WIDTH)
    handed, = call(hand_kernel, [(grad_out, BF16)], [], cat_up, w_low, w_select, core)
    above = lax.ppermute(handed, "ly", [(1, 0)])
    held_cat, _ = lax.optimization_barrier((cat, handed))
    early = (x, side, held_cat, w_delta, const)
    ahead = call(
        functools.partial(ahead_kernel, *dims), [(slab, F32), ((2 * tokens, 2 * doubled), BF16)] + [(shape, F32) for shape in state[4:]],
        [rows_all] + [pltpu.VMEM(a.shape, a.dtype) for a in early] + [pltpu.SemaphoreType.DMA((len(early),))],
        *early, far=len(early))

    send, core, dpre, rate_sum, end_sums = call(
        functools.partial(lower_kernel, *dims),
        [send_out, (grad_out, F32), (grad_out, BF16), ((states, 2 * micro, 128), F32), ((2, 2 * micro, 128), F32)],
        scratch + state[:3] + [pltpu.VMEM(w_delta.shape, BF16), pltpu.SemaphoreType.DMA((1,))], w_delta, above, *ahead, far=1)
    down_cat = to_all(scattered_sum(send, NEAR).astype(BF16), NEAR).reshape(tokens, WIDTH)

    own, deep = channels // replicas, rank // replicas
    lanes = own // TILE * rank + deep // TILE * channels + 128
    groups = lax.axis_size("zl")
    share_out = ((groups, TILE, lanes), BF16)
    keep, give = call(
        functools.partial(part_kernel, micro), [share_out, share_out], [(replicas, TILE, 128)],
        cat, down_cat, x, dpre, rate_sum, end_sums)
    other = lax.ppermute(give, "core", [(0, 1), (1, 0)])
    held_cat, _ = lax.optimization_barrier((down_cat, give))
    grad, = call(
        functools.partial(order_kernel, states), [((micro, length, channels), BF16)], [],
        const, held_cat, w_low, w_select, core)
    other, grad = lax.optimization_barrier((other, grad))
    pairs = (keep.astype(F32) + other.astype(F32)).astype(BF16)
    got = exchange(pairs, "zl")
    sums = call(
        total_kernel,
        [((own, rank), F32), ((deep, channels), F32), ((doubled // replicas, channels), F32),
         ((states // replicas, channels), F32), ((1, own), F32), ((1, own), F32)], [], got)
    return (grad, *sums[:4], sums[4].reshape(own), sums[5].reshape(own))


def solution(mesh):
    axes = ("ly", "yl", "zh", "x") + REPLICAS
    fine = Mesh(np.asarray(mesh.devices).reshape(2, 2, 4, 4, 4, 2), axes)
    section, dp = axes[:4], REPLICAS
    in_specs = (
        P(None, dp, section),
        P(None, dp, section),
        P(),
        P(section, None),
        P(None, section),
        P(None, section),
        P(None, section),
        P(section),
        P(section),
    )
    out_specs = (
        P(None, dp, section),
        P(section + dp, None),
        P(dp, section),
        P(dp, section),
        P(dp, section),
        P(section + dp),
        P(section + dp),
    )
    return jax.shard_map(per_device, mesh=fine, in_specs=in_specs, out_specs=out_specs, check_vma=False)
```

```python
import functools

import jax
import jax.numpy as jnp
import numpy as np
from jax import lax
from jax.experimental import pallas as pl
from jax.experimental.pallas import tpu as pltpu
from jax.sharding import Mesh
from jax.sharding import PartitionSpec as P

F32, BF16 = jnp.float32, jnp.bfloat16
WIDTH = 640
NN = (((1,), (0,)), ((), ()))
NT = (((1,), (1,)), ((), ()))
TN = (((0,), (0,)), ((), ()))
NEAR = ("yl", "x")
REPLICAS = ("zl", "core")
VMEM_LIMIT = 24 * 1024 * 1024
PROJECT_LIMIT = 60 * 1024 * 1024
SEL_ROWS = 8
TILE = 16


def dot(a, b, dims=NN):
    return lax.dot_general(a, b, dims, preferred_element_type=F32)


def iota(shape, dim):
    return lax.broadcasted_iota(jnp.int32, shape, dim)


def one_hot(mask):
    return jnp.where(mask, 1.0, 0.0).astype(BF16)


def spread_matrix(micro, length):
    shape = (2 * micro * length, micro * length)
    r, c = iota(shape, 0), iota(shape, 1)
    return one_hot((r % micro) * length + r // (2 * micro) == c)


def gather_matrix(micro, length):
    shape = (micro * length, 2 * micro * length)
    r, c = iota(shape, 0), iota(shape, 1)
    return one_hot(r == (c % micro) * length + c // (2 * micro))


def first_half(rows, micro, lanes=128):
    return (iota((rows, lanes), 0) // micro) % 2 == 0


def pick_half(half, wide):
    return jnp.where(half, wide[:, :128], wide[:, 128:])


def two_halves(half, value):
    return jnp.concatenate([jnp.where(half, value, 0.0), jnp.where(half, 0.0, value)], axis=1)


def two_terms(value):
    high = value.astype(BF16)
    return high, (value - high.astype(F32)).astype(BF16)


def fetch(sources, targets, sems):
    copies = [pltpu.make_async_copy(src, dst, sems.at[i]) for i, (src, dst) in enumerate(zip(sources, targets))]
    for copy in copies:
        copy.start()
    return copies


def project_kernel(x_hbm, ws_hbm, wl_hbm, rate_hbm, bias_hbm, skip_hbm, plan_hbm, out_ref, const_ref,
                   x_ref, ws_ref, wl_ref, rate_ref, bias_ref, skip_ref, plan_ref, sems):
    copies = fetch((x_hbm, wl_hbm, ws_hbm, rate_hbm, bias_hbm, skip_hbm, plan_hbm),
                   (x_ref, wl_ref, ws_ref, rate_ref, bias_ref, skip_ref, plan_ref), sems)
    rank, doubled, states = wl_ref.shape[1], ws_ref.shape[0], rate_ref.shape[0]
    const_ref[...] = jnp.zeros(const_ref.shape, F32)
    out_ref[:, rank:] = jnp.zeros((x_ref.shape[0], WIDTH - rank), BF16)
    for copy in copies:
        copy.wait()
    x = x_ref[...]
    out_ref[:, :rank] = dot(x, wl_ref[...]).astype(BF16)
    out_ref[:, rank:rank + doubled] = dot(x, ws_ref[...], NT).astype(BF16)
    const_ref[:states, :] = rate_ref[...]
    const_ref[states:states + 1, :] = bias_ref[...]
    const_ref[states + 1:states + 2, :] = skip_ref[...]
    for j in range(plan_ref.shape[0]):
        at = states + 2 + j
        const_ref[at:at + 1, :] = jnp.full((1, const_ref.shape[1]), plan_ref[j], jnp.int32).astype(F32)


def state_lanes(states):
    shape = (2 * states, 2 * states * 128)
    return one_hot(iota(shape, 1) // 128 == iota(shape, 0))


def grouped_sums(value, count, group=8):
    shape = (group * 128, group)
    ones = one_hot(iota(shape, 0) // 128 == iota(shape, 1))
    parts = [dot(value[:, at * 128:(at + group) * 128], ones) for at in range(0, count, group)]
    return jnp.concatenate(parts, axis=1)


def put_rows(ref, micro, value):
    length = value.shape[0] // micro
    for k in range(2):
        for m in range(micro):
            ref[pl.ds(k * micro + m, length, stride=2 * micro), :] = value[m * length:(m + 1) * length, k * 128:(k + 1) * 128]


def get_rows(ref, micro):
    length = ref.shape[0] // (2 * micro) - 1
    return jnp.concatenate([jnp.concatenate(
        [ref[pl.ds(k * micro + m, length, stride=2 * micro), :] for m in range(micro)], axis=0)
        for k in range(2)], axis=1)


def prepare(micro, length, states, rank, x, cat, wd, const_ref, DP, Q, R, X, D, DX, SG):
    rows = 2 * micro * length
    doubled = 2 * states
    half = first_half(rows, micro)
    lower = first_half(2 * micro, micro)
    T = spread_matrix(micro, length)
    slabs = (length, 2 * micro, 128)
    cat8 = dot(T, cat[:, rank:rank + 2 * doubled]).astype(BF16)
    x8 = pick_half(half, dot(T, x)).reshape(slabs)
    Q[...] = cat8
    put_rows(DP, micro, dot(cat[:, :rank], wd))
    pre8 = DP[:2 * micro * length, :].reshape(slabs)
    pre8 = pre8 + pick_half(lower, const_ref[states:states + 1, :])[None]
    step8 = jax.nn.softplus(pre8)
    X[...] = x8
    D[...] = step8
    DX[...] = step8 * x8
    SG[...] = jax.nn.sigmoid(pre8)
    for n in range(states):
        R[n] = pick_half(lower, const_ref[n:n + 1, :])
    R[states] = pick_half(lower, const_ref[states + 1:states + 2, :])


def forward(micro, length, states, A, H, BC, Q, R, X, D, DX, SG):
    pick = state_lanes(states)
    BC[...] = dot(Q[...], jnp.concatenate([pick, pick], axis=0)).reshape(BC.shape)
    zero = jnp.zeros((2 * micro, 128), F32)
    for n in range(states):
        H[0, n] = zero

    def ahead(t, h):
        d, dx = D[t], DX[t]
        out = []
        for n in range(states):
            a = jnp.exp(-(d * R[n]))
            h_n = a * h[n] + dx * BC[t, :, n * 128:(n + 1) * 128]
            A[t, n] = a
            H[t + 1, n] = h_n
            out.append(h_n)
        return tuple(out)

    lax.fori_loop(0, length, ahead, (zero,) * states, unroll=length)


def backward(micro, length, states, rank, sums, wd_ref, copies, G, A, H, BC, Q, R, X, D, DX, SG,
             send_ref, core_ref, products, DP, C):
    rows = 2 * micro * length
    doubled = 2 * states
    half = first_half(rows, micro)
    zero = jnp.zeros((2 * micro, 128), F32)
    skip8 = R[states]

    def back(i, carry):
        later, bias_acc, skip_acc = carry
        pair = length // 2 - 1 - i
        times = (2 * pair, 2 * pair + 1)
        d, dx, g, xv = ([ref[t] for t in times] for ref in (D, DX, G, X))
        u, w = [zero, zero], [zero, zero]
        passed = []
        for n in range(states):
            rate = R[n]
            b_at, c_at = (slice(at * 128, (at + 1) * 128) for at in (n, states + n))
            h = [H[times[0] + k, n] for k in range(3)]
            lam, q = [None, None], [None, None]
            through = later[n]
            for k in (1, 0):
                lam[k] = BC[times[k], :, c_at] * g[k] + through
                through = A[times[k], n] * lam[k]
                q[k] = through * h[k]
                u[k] = u[k] + lam[k] * BC[times[k], :, b_at]
                w[k] = w[k] + q[k] * rate
            for at, value in ((b_at, [lam[k] * dx[k] for k in range(2)]),
                              (c_at, [g[k] * h[k + 1] for k in range(2)])):
                products[pair, :, at] = jnp.concatenate(value, axis=0).astype(BF16)
            passed.append(through)
            if sums is not None:
                sums[n] = sums[n] + (d[0] * q[0] + d[1] * q[1])
        for k in range(2):
            dpre = (u[k] * xv[k] - w[k]) * SG[times[k]]
            DP[pl.ds(times[k] * 2 * micro, 2 * micro), :] = dpre
            C[pl.ds(times[k] * 2 * micro, 2 * micro), :] = g[k] + (u[k] * d[k] + skip8 * g[k])
            if sums is not None:
                bias_acc, skip_acc = bias_acc + dpre, skip_acc + g[k] * xv[k]
        return tuple(passed), bias_acc, skip_acc

    if sums is not None:
        sums[...] = jnp.zeros(sums.shape, F32)
    start = ((zero,) * states, zero, zero)
    _, bias_acc, skip_acc = lax.fori_loop(0, length // 2, back, start, unroll=length // 2)
    S = gather_matrix(micro, length)
    core_ref[...] = get_rows(C, micro)
    dpre_half = get_rows(DP, micro).astype(BF16)
    for copy in copies:
        copy.wait()
    send_ref[:, :rank] = dot(dpre_half, wd_ref[...], NT).astype(BF16)
    high, low = two_terms(grouped_sums(products[...].reshape(rows, doubled * 128), doubled))
    send_ref[:, rank:] = jnp.zeros((micro * length, WIDTH - rank), BF16)
    send_ref[:, rank:rank + doubled] = (dot(S, high) + dot(S, low)).astype(BF16)
    return dpre_half, bias_acc, skip_acc


def spread_rows(micro, length, ref):
    half = first_half(2 * micro * length, micro)
    return pick_half(half, dot(spread_matrix(micro, length), ref[...])).reshape(length, 2 * micro, 128)


def upper_kernel(micro, length, states, rank, x_ref, side_ref, cat_ref, wd_ref, const_ref, send_ref, core_ref,
                 G, products, DP, C, *state):
    G[...] = spread_rows(micro, length, side_ref)
    prepare(micro, length, states, rank, x_ref[...], cat_ref[...], wd_ref[...], const_ref, DP, *state[3:])
    forward(micro, length, states, *state)
    backward(micro, length, states, rank, None, wd_ref, (), G, *state, send_ref, core_ref, products, DP, C)


def ahead_kernel(micro, length, states, rank, x_any, side_any, cat_any, wd_any, const_any, *refs):
    *outs, DP, x_ref, side_ref, cat_ref, wd_ref, const_ref, sems = refs
    for copy in fetch((x_any, side_any, cat_any, wd_any, const_any), (x_ref, side_ref, cat_ref, wd_ref, const_ref), sems):
        copy.wait()
    outs[0][...] = spread_rows(micro, length, side_ref)
    prepare(micro, length, states, rank, x_ref[...], cat_ref[...], wd_ref[...], const_ref, DP, *outs[1:])


def lower_kernel(micro, length, states, rank, wd_any, above_ref, side_ref, *refs):
    *ready, send_ref, core_ref, dpre_ref, rate_ref, ends_ref, G, products, DP, C, A, H, BC, wd_ref, sems = refs
    state = (A, H, BC, *ready)
    copies = fetch((wd_any,), (wd_ref,), sems)
    G[...] = side_ref[...] + spread_rows(micro, length, above_ref)
    forward(micro, length, states, *state)
    dpre_half, bias_acc, skip_acc = backward(
        micro, length, states, rank, rate_ref, wd_ref, copies, G, *state, send_ref, core_ref, products, DP, C)
    dpre_ref[...] = dpre_half
    ends_ref[0] = bias_acc
    ends_ref[1] = skip_acc


def layer_grad(cat_ref, wl_ref, ws_ref, core_ref):
    rank, doubled = wl_ref.shape[1], ws_ref.shape[0]
    value = core_ref[...] + dot(cat_ref[:, :rank], wl_ref[...], NT)
    return (value + dot(cat_ref[:, rank:rank + doubled], ws_ref[...])).astype(BF16)


def hand_kernel(cat_ref, wl_ref, ws_ref, core_ref, grad_ref):
    grad_ref[...] = layer_grad(cat_ref, wl_ref, ws_ref, core_ref)


def part_kernel(micro, cat_ref, down_ref, x_ref, dpre_ref, rate_ref, ends_ref, keep_ref, give_ref, small):
    groups, tile, _ = keep_ref.shape
    cores = small.shape[0] // groups
    replicas, states = cores * groups, rate_ref.shape[0]
    channels, rank = x_ref.shape[1], cat_ref.shape[1] // 128 * 128 - 128
    own, deep, doubled = channels // replicas, rank // replicas, 2 * states
    share, rate_share = doubled // replicas, states // replicas
    x, down = x_ref[...], down_ref[...]
    low = dot(x, down[:, :rank], TN).astype(BF16)
    delta = dot(cat_ref[:, :rank], dpre_ref[...], TN).astype(BF16)
    select = dot(down[:, rank:rank + doubled], x, TN)
    lower = first_half(2 * micro, micro)

    def row_of(value):
        return jnp.sum(two_halves(lower, value), axis=0, keepdims=True)

    small[...] = jnp.zeros(small.shape, F32)
    for r in range(replicas):
        for k in range(2):
            small[r, k * share:(k + 1) * share, :] = select[r * share:(r + 1) * share, k * 128:(k + 1) * 128]
    for n in range(states):
        row = -row_of(rate_ref[n])
        at = SEL_ROWS + 2 * (n % rate_share)
        small[n // rate_share, at:at + 1, :] = row[:, :128]
        small[n // rate_share, at + 1:at + 2, :] = row[:, 128:]
    at = SEL_ROWS + 2 * rate_share
    for k in range(2):
        row = row_of(ends_ref[k])
        for r in range(replicas):
            small[r, at + k:at + k + 1, :own] = row[:, r * own:(r + 1) * own]
    first = own // tile * rank

    def fill(ref, core):
        for z in range(groups):
            r = z * cores + core
            for i in range(own // tile):
                ref[z, :, i * rank:(i + 1) * rank] = low[r * own + i * tile:r * own + (i + 1) * tile]
            for i in range(deep // tile):
                lanes = slice(first + i * channels, first + (i + 1) * channels)
                ref[z, :, lanes] = delta[r * deep + i * tile:r * deep + (i + 1) * tile]
            ref[z, :, first + deep // tile * channels:] = small[r].astype(BF16)

    mine = lax.axis_index("core")
    for core in range(cores):
        @pl.when(mine == core)
        def _():
            fill(keep_ref, core)
            fill(give_ref, 1 - core)


def order_kernel(states, const_ref, down_ref, wl_ref, ws_ref, core_ref, grad_ref):
    micro = grad_ref.shape[0]
    grad = layer_grad(down_ref, wl_ref, ws_ref, core_ref).astype(F32).reshape(grad_ref.shape)
    for j in range(micro):
        which = const_ref[states + 2 + j:states + 3 + j, :]
        value = grad[0]
        for m in range(1, micro):
            value = jnp.where(which == float(m), grad[m], value)
        grad_ref[j] = value.astype(BF16)


def total_kernel(got_ref, low_ref, delta_ref, sel_ref, rate_ref, bias_ref, skip_ref):
    tile = got_ref.shape[1]
    own, rank = low_ref.shape
    deep, channels = delta_ref.shape

    def summed(start, lanes):
        value = got_ref[0, :, start:start + lanes].astype(F32)
        for r in range(1, got_ref.shape[0]):
            value = value + got_ref[r, :, start:start + lanes].astype(F32)
        return value

    for i in range(own // tile):
        low_ref[i * tile:(i + 1) * tile] = summed(i * rank, rank)
    first = own // tile * rank
    for i in range(deep // tile):
        delta_ref[i * tile:(i + 1) * tile] = summed(first + i * channels, channels)
    small = summed(first + deep // tile * channels, 128)
    rows, share = sel_ref.shape[0], rate_ref.shape[0]
    for k in range(2):
        lanes = slice(k * 128, (k + 1) * 128)
        sel_ref[:, lanes] = small[k * rows:(k + 1) * rows]
        for n in range(share):
            at = SEL_ROWS + 2 * n + k
            rate_ref[n:n + 1, lanes] = small[at:at + 1]
    at = SEL_ROWS + 2 * share
    bias_ref[...] = small[at:at + 1, :own]
    skip_ref[...] = small[at + 1:at + 2, :own]


def call(kernel, outs, scratch, *args, far=0, limit=VMEM_LIMIT):
    vmem = pl.BlockSpec(memory_space=pltpu.VMEM)
    hbm = pl.BlockSpec(memory_space=pl.ANY)
    return pl.pallas_call(
        kernel,
        out_shape=[jax.ShapeDtypeStruct(*out) for out in outs],
        in_specs=[hbm] * far + [vmem] * (len(args) - far),
        out_specs=[vmem] * len(outs),
        scratch_shapes=[pltpu.VMEM(s, F32) if isinstance(s, tuple) else s for s in scratch],
        compiler_params=pltpu.CompilerParams(vmem_limit_bytes=limit),
    )(*args)


def exchange(blocks, axes):
    return lax.all_to_all(blocks, axes, 0, 0)


def to_all(block, axes):
    count = lax.axis_size(axes)
    return exchange(jnp.broadcast_to(block[None], (count,) + block.shape), axes)


def total(blocks):
    return jnp.sum(blocks.astype(F32), axis=0)


def scattered_sum(rows, axes):
    count = lax.axis_size(axes)
    got = exchange(rows.reshape(count, rows.shape[0] // count, rows.shape[1]), axes)
    return total(to_all(total(got).astype(BF16), "zh"))


def per_device(x_saved, side_grad, plan, w_low, w_delta, w_select, decay_rate, delta_bias, skip_gain):
    micro, length, channels = x_saved.shape
    tokens = micro * length
    rank, doubled, states = w_low.shape[1], w_select.shape[0], decay_rate.shape[0]
    replicas = lax.axis_size(REPLICAS)
    x = x_saved.reshape(tokens, channels)
    side = side_grad.reshape(tokens, channels)
    bias, skip = delta_bias.reshape(1, channels), skip_gain.reshape(1, channels)

    sources = (x, w_select, w_low, decay_rate, bias, skip, plan)
    part, const = call(
        project_kernel, [((tokens, WIDTH), BF16), ((states + 8, channels), F32)],
        [pltpu.VMEM(a.shape, a.dtype) for a in sources[:-1]]
        + [pltpu.SMEM(plan.shape, plan.dtype), pltpu.SemaphoreType.DMA((len(sources),))],
        *sources, far=len(sources), limit=PROJECT_LIMIT)
    summed = scattered_sum(part, NEAR)
    selected = summed[:, rank:rank + doubled]
    high = lax.reduce_precision(selected, 8, 7)
    rest = summed[:, rank + 2 * doubled:]
    packed = jnp.concatenate([summed[:, :rank], high, selected - high, rest], axis=1).astype(BF16)
    cat = to_all(packed, NEAR).reshape(tokens, WIDTH)

    dims = (micro, length, states, rank)
    slab, rows_all = (length, 2 * micro, 128), (2 * tokens + 2 * micro, 128)
    send_out, grad_out = ((tokens, WIDTH), BF16), (tokens, channels)
    scratch = [slab, pltpu.VMEM((length // 2, 4 * micro, doubled * 128), BF16), rows_all, rows_all]
    state = [(length, states, 2 * micro, 128), (length + 1, states, 2 * micro, 128),
             (length, 2 * micro, doubled * 128), (states + 1, 2 * micro, 128), slab, slab, slab, slab]
    state.insert(3, pltpu.VMEM((2 * tokens, 2 * doubled), BF16))
    send, core = call(
        functools.partial(upper_kernel, *dims), [send_out, (grad_out, F32)], scratch + state,
        x, side, cat, w_delta, const)
    cat_up = to_all(scattered_sum(send, NEAR).astype(BF16), NEAR).reshape(tokens, WIDTH)
    handed, = call(hand_kernel, [(grad_out, BF16)], [], cat_up, w_low, w_select, core)
    above = lax.ppermute(handed, "ly", [(1, 0)])
    held_cat, _ = lax.optimization_barrier((cat, handed))
    early = (x, side, held_cat, w_delta, const)
    ahead = call(
        functools.partial(ahead_kernel, *dims), [(slab, F32), ((2 * tokens, 2 * doubled), BF16)] + [(shape, F32) for shape in state[4:]],
        [rows_all] + [pltpu.VMEM(a.shape, a.dtype) for a in early] + [pltpu.SemaphoreType.DMA((len(early),))],
        *early, far=len(early))

    send, core, dpre, rate_sum, end_sums = call(
        functools.partial(lower_kernel, *dims),
        [send_out, (grad_out, F32), (grad_out, BF16), ((states, 2 * micro, 128), F32), ((2, 2 * micro, 128), F32)],
        scratch + state[:3] + [pltpu.VMEM(w_delta.shape, BF16), pltpu.SemaphoreType.DMA((1,))], w_delta, above, *ahead, far=1)
    down_cat = to_all(scattered_sum(send, NEAR).astype(BF16), NEAR).reshape(tokens, WIDTH)

    own, deep = channels // replicas, rank // replicas
    lanes = own // TILE * rank + deep // TILE * channels + 128
    groups = lax.axis_size("zl")
    share_out = ((groups, TILE, lanes), BF16)
    keep, give = call(
        functools.partial(part_kernel, micro), [share_out, share_out], [(replicas, TILE, 128)],
        cat, down_cat, x, dpre, rate_sum, end_sums)
    other = lax.ppermute(give, "core", [(0, 1), (1, 0)])
    held_cat, _ = lax.optimization_barrier((down_cat, give))
    grad, = call(
        functools.partial(order_kernel, states), [((micro, length, channels), BF16)], [],
        const, held_cat, w_low, w_select, core)
    other, grad = lax.optimization_barrier((other, grad))
    pairs = (keep.astype(F32) + other.astype(F32)).astype(BF16)
    got = exchange(pairs, "zl")
    sums = call(
        total_kernel,
        [((own, rank), F32), ((deep, channels), F32), ((doubled // replicas, channels), F32),
         ((states // replicas, channels), F32), ((1, own), F32), ((1, own), F32)], [], got)
    return (grad, *sums[:4], sums[4].reshape(own), sums[5].reshape(own))


def solution(mesh):
    axes = ("ly", "yl", "zh", "x") + REPLICAS
    fine = Mesh(np.asarray(mesh.devices).reshape(2, 2, 4, 4, 4, 2), axes)
    section, dp = axes[:4], REPLICAS
    in_specs = (
        P(None, dp, section),
        P(None, dp, section),
        P(),
        P(section, None),
        P(None, section),
        P(None, section),
        P(None, section),
        P(section),
        P(section),
    )
    out_specs = (
        P(None, dp, section),
        P(section + dp, None),
        P(dp, section),
        P(dp, section),
        P(dp, section),
        P(section + dp),
        P(section + dp),
    )
    return jax.shard_map(per_device, mesh=fine, in_specs=in_specs, out_specs=out_specs, check_vma=False)
```

```python
import functools

import jax
import jax.numpy as jnp
import numpy as np
from jax import lax
from jax.experimental import pallas as pl
from jax.experimental.pallas import tpu as pltpu
from jax.sharding import Mesh
from jax.sharding import PartitionSpec as P

F32, BF16 = jnp.float32, jnp.bfloat16
WIDTH = 640
NN = (((1,), (0,)), ((), ()))
NT = (((1,), (1,)), ((), ()))
TN = (((0,), (0,)), ((), ()))
NEAR = ("yl", "x")
REPLICAS = ("zl", "core")
VMEM_LIMIT = 24 * 1024 * 1024
PROJECT_LIMIT = 60 * 1024 * 1024
SEL_ROWS = 8
TILE = 16


def dot(a, b, dims=NN):
    return lax.dot_general(a, b, dims, preferred_element_type=F32)


def iota(shape, dim):
    return lax.broadcasted_iota(jnp.int32, shape, dim)


def one_hot(mask):
    return jnp.where(mask, 1.0, 0.0).astype(BF16)


def spread_matrix(micro, length):
    shape = (2 * micro * length, micro * length)
    r, c = iota(shape, 0), iota(shape, 1)
    return one_hot((r % micro) * length + r // (2 * micro) == c)


def gather_matrix(micro, length):
    shape = (micro * length, 2 * micro * length)
    r, c = iota(shape, 0), iota(shape, 1)
    return one_hot(r == (c % micro) * length + c // (2 * micro))


def first_half(rows, micro, lanes=128):
    return (iota((rows, lanes), 0) // micro) % 2 == 0


def pick_half(half, wide):
    return jnp.where(half, wide[:, :128], wide[:, 128:])


def two_halves(half, value):
    return jnp.concatenate([jnp.where(half, value, 0.0), jnp.where(half, 0.0, value)], axis=1)


def two_terms(value):
    high = value.astype(BF16)
    return high, (value - high.astype(F32)).astype(BF16)


def fetch(sources, targets, sems):
    copies = [pltpu.make_async_copy(src, dst, sems.at[i]) for i, (src, dst) in enumerate(zip(sources, targets))]
    for copy in copies:
        copy.start()
    return copies


def project_kernel(x_hbm, ws_hbm, wl_hbm, rate_hbm, bias_hbm, skip_hbm, plan_hbm, out_ref, const_ref,
                   x_ref, ws_ref, wl_ref, rate_ref, bias_ref, skip_ref, plan_ref, sems):
    copies = fetch((x_hbm, wl_hbm, ws_hbm, rate_hbm, bias_hbm, skip_hbm, plan_hbm),
                   (x_ref, wl_ref, ws_ref, rate_ref, bias_ref, skip_ref, plan_ref), sems)
    rank, doubled, states = wl_ref.shape[1], ws_ref.shape[0], rate_ref.shape[0]
    const_ref[...] = jnp.zeros(const_ref.shape, F32)
    out_ref[:, rank:] = jnp.zeros((x_ref.shape[0], WIDTH - rank), BF16)
    for copy in copies:
        copy.wait()
    x = x_ref[...]
    out_ref[:, :rank] = dot(x, wl_ref[...]).astype(BF16)
    out_ref[:, rank:rank + doubled] = dot(x, ws_ref[...], NT).astype(BF16)
    const_ref[:states, :] = rate_ref[...]
    const_ref[states:states + 1, :] = bias_ref[...]
    const_ref[states + 1:states + 2, :] = skip_ref[...]
    for j in range(plan_ref.shape[0]):
        at = states + 2 + j
        const_ref[at:at + 1, :] = jnp.full((1, const_ref.shape[1]), plan_ref[j], jnp.int32).astype(F32)


def state_lanes(states):
    shape = (2 * states, 2 * states * 128)
    return one_hot(iota(shape, 1) // 128 == iota(shape, 0))


def grouped_sums(value, count, group=8):
    shape = (group * 128, group)
    ones = one_hot(iota(shape, 0) // 128 == iota(shape, 1))
    parts = [dot(value[:, at * 128:(at + group) * 128], ones) for at in range(0, count, group)]
    return jnp.concatenate(parts, axis=1)


def put_rows(ref, micro, value):
    length = value.shape[0] // micro
    for k in range(2):
        for m in range(micro):
            ref[pl.ds(k * micro + m, length, stride=2 * micro), :] = value[m * length:(m + 1) * length, k * 128:(k + 1) * 128]


def get_rows(ref, micro):
    length = ref.shape[0] // (2 * micro) - 1
    return jnp.concatenate([jnp.concatenate(
        [ref[pl.ds(k * micro + m, length, stride=2 * micro), :] for m in range(micro)], axis=0)
        for k in range(2)], axis=1)


def prepare(micro, length, states, rank, x, cat, wd, const_ref, DP, Q, R, X, D, DX, SG):
    rows = 2 * micro * length
    doubled = 2 * states
    half = first_half(rows, micro)
    lower = first_half(2 * micro, micro)
    T = spread_matrix(micro, length)
    slabs = (length, 2 * micro, 128)
    cat8 = dot(T, cat[:, rank:rank + 2 * doubled]).astype(BF16)
    x8 = pick_half(half, dot(T, x)).reshape(slabs)
    Q[...] = cat8
    put_rows(DP, micro, dot(cat[:, :rank], wd))
    pre8 = DP[:2 * micro * length, :].reshape(slabs)
    pre8 = pre8 + pick_half(lower, const_ref[states:states + 1, :])[None]
    step8 = jax.nn.softplus(pre8)
    X[...] = x8
    D[...] = step8
    DX[...] = step8 * x8
    SG[...] = jax.nn.sigmoid(pre8)
    for n in range(states):
        R[n] = pick_half(lower, const_ref[n:n + 1, :])
    R[states] = pick_half(lower, const_ref[states + 1:states + 2, :])


def forward(micro, length, states, A, H, BC, Q, R, X, D, DX, SG):
    pick = state_lanes(states)
    BC[...] = dot(Q[...], jnp.concatenate([pick, pick], axis=0)).reshape(BC.shape)
    zero = jnp.zeros((2 * micro, 128), F32)
    for n in range(states):
        H[0, n] = zero

    def ahead(t, h):
        d, dx = D[t], DX[t]
        out = []
        for n in range(states):
            a = jnp.exp(-(d * R[n]))
            h_n = a * h[n] + dx * BC[t, :, n * 128:(n + 1) * 128]
            A[t, n] = a
            H[t + 1, n] = h_n
            out.append(h_n)
        return tuple(out)

    lax.fori_loop(0, length, ahead, (zero,) * states, unroll=length)


def backward(micro, length, states, rank, sums, wd_ref, copies, G, A, H, BC, Q, R, X, D, DX, SG,
             send_ref, core_ref, products, DP, C):
    rows = 2 * micro * length
    doubled = 2 * states
    half = first_half(rows, micro)
    zero = jnp.zeros((2 * micro, 128), F32)
    skip8 = R[states]

    def back(i, carry):
        later, bias_acc, skip_acc = carry
        pair = length // 2 - 1 - i
        times = (2 * pair, 2 * pair + 1)
        d, dx, g, xv = ([ref[t] for t in times] for ref in (D, DX, G, X))
        u, w = [zero, zero], [zero, zero]
        passed = []
        for n in range(states):
            rate = R[n]
            b_at, c_at = (slice(at * 128, (at + 1) * 128) for at in (n, states + n))
            h = [H[times[0] + k, n] for k in range(3)]
            lam, q = [None, None], [None, None]
            through = later[n]
            for k in (1, 0):
                lam[k] = BC[times[k], :, c_at] * g[k] + through
                through = A[times[k], n] * lam[k]
                q[k] = through * h[k]
                u[k] = u[k] + lam[k] * BC[times[k], :, b_at]
                w[k] = w[k] + q[k] * rate
            for at, value in ((b_at, [lam[k] * dx[k] for k in range(2)]),
                              (c_at, [g[k] * h[k + 1] for k in range(2)])):
                products[pair, :, at] = jnp.concatenate(value, axis=0).astype(BF16)
            passed.append(through)
            if sums is not None:
                sums[n] = sums[n] + (d[0] * q[0] + d[1] * q[1])
        for k in range(2):
            dpre = (u[k] * xv[k] - w[k]) * SG[times[k]]
            DP[pl.ds(times[k] * 2 * micro, 2 * micro), :] = dpre
            C[pl.ds(times[k] * 2 * micro, 2 * micro), :] = g[k] + (u[k] * d[k] + skip8 * g[k])
            if sums is not None:
                bias_acc, skip_acc = bias_acc + dpre, skip_acc + g[k] * xv[k]
        return tuple(passed), bias_acc, skip_acc

    if sums is not None:
        sums[...] = jnp.zeros(sums.shape, F32)
    start = ((zero,) * states, zero, zero)
    _, bias_acc, skip_acc = lax.fori_loop(0, length // 2, back, start, unroll=length // 2)
    S = gather_matrix(micro, length)
    core_ref[...] = get_rows(C, micro)
    dpre_half = get_rows(DP, micro).astype(BF16)
    for copy in copies:
        copy.wait()
    send_ref[:, :rank] = dot(dpre_half, wd_ref[...], NT).astype(BF16)
    high, low = two_terms(grouped_sums(products[...].reshape(rows, doubled * 128), doubled))
    send_ref[:, rank:] = jnp.zeros((micro * length, WIDTH - rank), BF16)
    send_ref[:, rank:rank + doubled] = (dot(S, high) + dot(S, low)).astype(BF16)
    return dpre_half, bias_acc, skip_acc


def spread_rows(micro, length, ref):
    half = first_half(2 * micro * length, micro)
    return pick_half(half, dot(spread_matrix(micro, length), ref[...])).reshape(length, 2 * micro, 128)


def upper_kernel(micro, length, states, rank, x_ref, side_ref, cat_ref, wd_ref, const_ref, send_ref, core_ref,
                 G, products, DP, C, *state):
    G[...] = spread_rows(micro, length, side_ref)
    prepare(micro, length, states, rank, x_ref[...], cat_ref[...], wd_ref[...], const_ref, DP, *state[3:])
    forward(micro, length, states, *state)
    backward(micro, length, states, rank, None, wd_ref, (), G, *state, send_ref, core_ref, products, DP, C)


def ahead_kernel(micro, length, states, rank, x_any, side_any, cat_any, wd_any, const_any, *refs):
    *outs, DP, x_ref, side_ref, cat_ref, wd_ref, const_ref, sems = refs
    for copy in fetch((x_any, side_any, cat_any, wd_any, const_any), (x_ref, side_ref, cat_ref, wd_ref, const_ref), sems):
        copy.wait()
    outs[0][...] = spread_rows(micro, length, side_ref)
    prepare(micro, length, states, rank, x_ref[...], cat_ref[...], wd_ref[...], const_ref, DP, *outs[1:])


def lower_kernel(micro, length, states, rank, wd_any, above_ref, side_ref, *refs):
    *ready, send_ref, core_ref, dpre_ref, rate_ref, ends_ref, G, products, DP, C, A, H, BC, wd_ref, sems = refs
    state = (A, H, BC, *ready)
    copies = fetch((wd_any,), (wd_ref,), sems)
    G[...] = side_ref[...] + spread_rows(micro, length, above_ref)
    forward(micro, length, states, *state)
    dpre_half, bias_acc, skip_acc = backward(
        micro, length, states, rank, rate_ref, wd_ref, copies, G, *state, send_ref, core_ref, products, DP, C)
    dpre_ref[...] = dpre_half
    ends_ref[0] = bias_acc
    ends_ref[1] = skip_acc


def layer_grad(cat_ref, wl_ref, ws_ref, core_ref):
    rank, doubled = wl_ref.shape[1], ws_ref.shape[0]
    value = core_ref[...] + dot(cat_ref[:, :rank], wl_ref[...], NT)
    return (value + dot(cat_ref[:, rank:rank + doubled], ws_ref[...])).astype(BF16)


def hand_kernel(cat_ref, wl_ref, ws_ref, core_ref, grad_ref):
    grad_ref[...] = layer_grad(cat_ref, wl_ref, ws_ref, core_ref)


def part_kernel(micro, away, cat_ref, down_ref, x_ref, dpre_ref, rate_ref, ends_ref, out_ref, small):
    groups, tile, _ = out_ref.shape
    cores = small.shape[0] // groups
    replicas, states = cores * groups, rate_ref.shape[0]
    channels, rank = x_ref.shape[1], cat_ref.shape[1] // 128 * 128 - 128
    own, deep, doubled = channels // replicas, rank // replicas, 2 * states
    share, rate_share = doubled // replicas, states // replicas
    x, down = x_ref[...], down_ref[...]
    low = dot(x, down[:, :rank], TN).astype(BF16)
    delta = dot(cat_ref[:, :rank], dpre_ref[...], TN).astype(BF16)
    select = dot(down[:, rank:rank + doubled], x, TN)
    lower = first_half(2 * micro, micro)

    def row_of(value):
        return jnp.sum(two_halves(lower, value), axis=0, keepdims=True)

    small[...] = jnp.zeros(small.shape, F32)
    for r in range(replicas):
        for k in range(2):
            small[r, k * share:(k + 1) * share, :] = select[r * share:(r + 1) * share, k * 128:(k + 1) * 128]
    for n in range(states):
        row = -row_of(rate_ref[n])
        at = SEL_ROWS + 2 * (n % rate_share)
        small[n // rate_share, at:at + 1, :] = row[:, :128]
        small[n // rate_share, at + 1:at + 2, :] = row[:, 128:]
    at = SEL_ROWS + 2 * rate_share
    for k in range(2):
        row = row_of(ends_ref[k])
        for r in range(replicas):
            small[r, at + k:at + k + 1, :own] = row[:, r * own:(r + 1) * own]
    first = own // tile * rank

    def fill(ref, core):
        for z in range(groups):
            r = z * cores + core
            for i in range(own // tile):
                ref[z, :, i * rank:(i + 1) * rank] = low[r * own + i * tile:r * own + (i + 1) * tile]
            for i in range(deep // tile):
                lanes = slice(first + i * channels, first + (i + 1) * channels)
                ref[z, :, lanes] = delta[r * deep + i * tile:r * deep + (i + 1) * tile]
            ref[z, :, first + deep // tile * channels:] = small[r].astype(BF16)

    mine = lax.axis_index("core")
    for core in range(cores):
        @pl.when(mine == core)
        def _():
            fill(out_ref, 1 - core if away else core)


def order_kernel(states, const_ref, down_ref, wl_ref, ws_ref, core_ref, grad_ref):
    micro = grad_ref.shape[0]
    grad = layer_grad(down_ref, wl_ref, ws_ref, core_ref).astype(F32).reshape(grad_ref.shape)
    for j in range(micro):
        which = const_ref[states + 2 + j:states + 3 + j, :]
        value = grad[0]
        for m in range(1, micro):
            value = jnp.where(which == float(m), grad[m], value)
        grad_ref[j] = value.astype(BF16)


def total_kernel(got_ref, low_ref, delta_ref, sel_ref, rate_ref, bias_ref, skip_ref):
    tile = got_ref.shape[1]
    own, rank = low_ref.shape
    deep, channels = delta_ref.shape

    def summed(start, lanes):
        value = got_ref[0, :, start:start + lanes].astype(F32)
        for r in range(1, got_ref.shape[0]):
            value = value + got_ref[r, :, start:start + lanes].astype(F32)
        return value

    for i in range(own // tile):
        low_ref[i * tile:(i + 1) * tile] = summed(i * rank, rank)
    first = own // tile * rank
    for i in range(deep // tile):
        delta_ref[i * tile:(i + 1) * tile] = summed(first + i * channels, channels)
    small = summed(first + deep // tile * channels, 128)
    rows, share = sel_ref.shape[0], rate_ref.shape[0]
    for k in range(2):
        lanes = slice(k * 128, (k + 1) * 128)
        sel_ref[:, lanes] = small[k * rows:(k + 1) * rows]
        for n in range(share):
            at = SEL_ROWS + 2 * n + k
            rate_ref[n:n + 1, lanes] = small[at:at + 1]
    at = SEL_ROWS + 2 * share
    bias_ref[...] = small[at:at + 1, :own]
    skip_ref[...] = small[at + 1:at + 2, :own]


def call(kernel, outs, scratch, *args, far=0, limit=VMEM_LIMIT):
    vmem = pl.BlockSpec(memory_space=pltpu.VMEM)
    hbm = pl.BlockSpec(memory_space=pl.ANY)
    return pl.pallas_call(
        kernel,
        out_shape=[jax.ShapeDtypeStruct(*out) for out in outs],
        in_specs=[hbm] * far + [vmem] * (len(args) - far),
        out_specs=[vmem] * len(outs),
        scratch_shapes=[pltpu.VMEM(s, F32) if isinstance(s, tuple) else s for s in scratch],
        compiler_params=pltpu.CompilerParams(vmem_limit_bytes=limit),
    )(*args)


def exchange(blocks, axes):
    return lax.all_to_all(blocks, axes, 0, 0)


def to_all(block, axes):
    count = lax.axis_size(axes)
    return exchange(jnp.broadcast_to(block[None], (count,) + block.shape), axes)


def total(blocks):
    return jnp.sum(blocks.astype(F32), axis=0)


def scattered_sum(rows, axes):
    count = lax.axis_size(axes)
    got = exchange(rows.reshape(count, rows.shape[0] // count, rows.shape[1]), axes)
    return total(to_all(total(got).astype(BF16), "zh"))


def per_device(x_saved, side_grad, plan, w_low, w_delta, w_select, decay_rate, delta_bias, skip_gain):
    micro, length, channels = x_saved.shape
    tokens = micro * length
    rank, doubled, states = w_low.shape[1], w_select.shape[0], decay_rate.shape[0]
    replicas = lax.axis_size(REPLICAS)
    x = x_saved.reshape(tokens, channels)
    side = side_grad.reshape(tokens, channels)
    bias, skip = delta_bias.reshape(1, channels), skip_gain.reshape(1, channels)

    sources = (x, w_select, w_low, decay_rate, bias, skip, plan)
    part, const = call(
        project_kernel, [((tokens, WIDTH), BF16), ((states + 8, channels), F32)],
        [pltpu.VMEM(a.shape, a.dtype) for a in sources[:-1]]
        + [pltpu.SMEM(plan.shape, plan.dtype), pltpu.SemaphoreType.DMA((len(sources),))],
        *sources, far=len(sources), limit=PROJECT_LIMIT)
    summed = scattered_sum(part, NEAR)
    selected = summed[:, rank:rank + doubled]
    high = lax.reduce_precision(selected, 8, 7)
    rest = summed[:, rank + 2 * doubled:]
    packed = jnp.concatenate([summed[:, :rank], high, selected - high, rest], axis=1).astype(BF16)
    cat = to_all(packed, NEAR).reshape(tokens, WIDTH)

    dims = (micro, length, states, rank)
    slab, rows_all = (length, 2 * micro, 128), (2 * tokens + 2 * micro, 128)
    send_out, grad_out = ((tokens, WIDTH), BF16), (tokens, channels)
    scratch = [slab, pltpu.VMEM((length // 2, 4 * micro, doubled * 128), BF16), rows_all, rows_all]
    state = [(length, states, 2 * micro, 128), (length + 1, states, 2 * micro, 128),
             (length, 2 * micro, doubled * 128), (states + 1, 2 * micro, 128), slab, slab, slab, slab]
    state.insert(3, pltpu.VMEM((2 * tokens, 2 * doubled), BF16))
    send, core = call(
        functools.partial(upper_kernel, *dims), [send_out, (grad_out, F32)], scratch + state,
        x, side, cat, w_delta, const)
    cat_up = to_all(scattered_sum(send, NEAR).astype(BF16), NEAR).reshape(tokens, WIDTH)
    handed, = call(hand_kernel, [(grad_out, BF16)], [], cat_up, w_low, w_select, core)
    above = lax.ppermute(handed, "ly", [(1, 0)])
    held_cat, _ = lax.optimization_barrier((cat, handed))
    early = (x, side, held_cat, w_delta, const)
    ahead = call(
        functools.partial(ahead_kernel, *dims), [(slab, F32), ((2 * tokens, 2 * doubled), BF16)] + [(shape, F32) for shape in state[4:]],
        [rows_all] + [pltpu.VMEM(a.shape, a.dtype) for a in early] + [pltpu.SemaphoreType.DMA((len(early),))],
        *early, far=len(early))

    send, core, dpre, rate_sum, end_sums = call(
        functools.partial(lower_kernel, *dims),
        [send_out, (grad_out, F32), (grad_out, BF16), ((states, 2 * micro, 128), F32), ((2, 2 * micro, 128), F32)],
        scratch + state[:3] + [pltpu.VMEM(w_delta.shape, BF16), pltpu.SemaphoreType.DMA((1,))], w_delta, above, *ahead, far=1)
    down_cat = to_all(scattered_sum(send, NEAR).astype(BF16), NEAR).reshape(tokens, WIDTH)

    own, deep = channels // replicas, rank // replicas
    lanes = own // TILE * rank + deep // TILE * channels + 128
    groups = lax.axis_size("zl")
    share_out = ((groups, TILE, lanes), BF16)
    give, = call(
        functools.partial(part_kernel, micro, True), [share_out], [(replicas, TILE, 128)],
        cat, down_cat, x, dpre, rate_sum, end_sums)
    other = lax.ppermute(give, "core", [(0, 1), (1, 0)])
    held_cat, _ = lax.optimization_barrier((down_cat, give))
    grad, = call(
        functools.partial(order_kernel, states), [((micro, length, channels), BF16)], [],
        const, held_cat, w_low, w_select, core)
    keep, = call(
        functools.partial(part_kernel, micro, False), [share_out], [(replicas, TILE, 128)],
        cat, held_cat, x, dpre, rate_sum, end_sums)
    other, grad, keep = lax.optimization_barrier((other, grad, keep))
    pairs = (keep.astype(F32) + other.astype(F32)).astype(BF16)
    got = exchange(pairs, "zl")
    sums = call(
        total_kernel,
        [((own, rank), F32), ((deep, channels), F32), ((doubled // replicas, channels), F32),
         ((states // replicas, channels), F32), ((1, own), F32), ((1, own), F32)], [], got)
    return (grad, *sums[:4], sums[4].reshape(own), sums[5].reshape(own))


def solution(mesh):
    axes = ("ly", "yl", "zh", "x") + REPLICAS
    fine = Mesh(np.asarray(mesh.devices).reshape(2, 2, 4, 4, 4, 2), axes)
    section, dp = axes[:4], REPLICAS
    in_specs = (
        P(None, dp, section),
        P(None, dp, section),
        P(),
        P(section, None),
        P(None, section),
        P(None, section),
        P(None, section),
        P(section),
        P(section),
    )
    out_specs = (
        P(None, dp, section),
        P(section + dp, None),
        P(dp, section),
        P(dp, section),
        P(dp, section),
        P(section + dp),
        P(section + dp),
    )
    return jax.shard_map(per_device, mesh=fine, in_specs=in_specs, out_specs=out_specs, check_vma=False)
```
